512 devices in a mesh: blk: 8 (over x, core), pair: 64 (over z, y).
Axes of the slice: x: 4, y: 8, z: 8, core: 2. Of those that a mesh axis runs over, the one named last changes fastest.
Arguments:
- source_points: float32 [3, 524288], P(None, 'blk'), may hold values from -5 to 5
- target_points: float32 [3, 524288], P(None, 'blk'), may hold values from -5 to 5
- source_logw: float32 [524288], P('blk'), may hold values from -4 to 4
- target_logw: float32 [524288], P('blk'), may hold values from -4 to 4
- warm_start: float32 [524288], P('blk'), may hold values from -4 to 112
- pairs: int32 [8, 64, 2, 40], P('blk', 'pair'), may hold values from -1 to 2047, as said below
- owner_slot: int32 [2048], replicated, may hold values from 0 to 2047, as said below
Outputs:
- source_pot: float32 [524288], P('blk')
- target_pot: float32 [524288], P('blk')
The draws below stay inside these ranges and needn't reach their ends.
Inputs may be any that keep to these rules, and one draw needn't show every extreme that they name: `pairs`: entry k of device (b, p) is empty (both rows -1) or live; live entries of each group of 5 positions come first, 1 to 5 of them, and some group of some device is full. A live source id s has s // 256 == b; a live target id t has owner_slot[t] // 256 == k // 5. `owner_slot`: A permutation of the storage slots.
All inputs are finite; a program needn't handle non-finite values.
Results may differ from the reference program's by a relative error of at most 0.0001.
Values sent between devices are 32-bit elements; how exact they have to be, the bound alone decides.
A program may use at most 128 MiB of HBM per device.

```python
import jax
import jax.numpy as jnp
from jax import lax

BS = 256
NB_DEV = 256
CAP = 5
ITERS = 2
POINTS = 524288
N_BLK = 8
N_PAIR = 64


def shared_order(key):
    return jax.random.permutation(jax.random.fold_in(key, 101), N_BLK * NB_DEV)


def draw_owner_slot(key, part):
    return shared_order(key).astype(jnp.int32)


def draw_pairs(key, part):
    order = shared_order(key).astype(jnp.int32)
    stored = jnp.argsort(order).astype(jnp.int32)
    key = jax.random.fold_in(key, 7)
    key_count, key_target, key_source, key_full = jax.random.split(key, 4)
    counts = jax.random.randint(key_count, (N_BLK * N_PAIR * N_BLK,), 1, CAP + 1)
    chosen = jax.random.randint(key_full, (), 0, N_BLK * N_PAIR * N_BLK)
    counts = jnp.where(jnp.arange(N_BLK * N_PAIR * N_BLK) == chosen, CAP, counts)
    counts = counts.reshape(N_BLK, N_PAIR, N_BLK, 1)
    position = jnp.arange(CAP).reshape(1, 1, 1, CAP)
    live = position < counts
    owner = jnp.arange(N_BLK).reshape(1, 1, N_BLK, 1)
    device = jnp.arange(N_BLK).reshape(N_BLK, 1, 1, 1)
    local_target = jax.random.randint(key_target, (N_BLK, N_PAIR, N_BLK, CAP), 0, NB_DEV)
    target_ids = stored[owner * NB_DEV + local_target]
    source_ids = device * NB_DEV + jax.random.randint(key_source, (N_BLK, N_PAIR, N_BLK, CAP), 0, NB_DEV)
    target_ids = jnp.where(live, target_ids, -1).reshape(N_BLK, N_PAIR, N_BLK * CAP)
    source_ids = jnp.where(live, source_ids, -1).reshape(N_BLK, N_PAIR, N_BLK * CAP)
    return jnp.stack((source_ids, target_ids), axis=2).astype(jnp.int32)


def draw_target_points(key, part):
    key = jax.random.fold_in(key, 31)
    key_spread = jax.random.fold_in(key, 0)
    return jnp.clip(jax.random.normal(key_spread, (3, N_BLK * NB_DEV * BS), jnp.float32), -5.0, 5.0)


def draw_warm_start(key, part):
    key = jax.random.fold_in(key, 23)
    key_base = jax.random.fold_in(key, 0)
    return jnp.clip(jax.random.normal(key_base, (N_BLK * NB_DEV * BS,), jnp.float32), -4.0, 4.0)


def shard_levels(rng, dims, pieces, least, largest):
    def one(dim, parts):
        steps = jax.random.uniform(jax.random.fold_in(jax.random.fold_in(rng, 6), dim), (parts,), jnp.float32, least / len(pieces), largest / len(pieces))
        return jnp.repeat(jnp.exp(steps), dims[dim] // parts).reshape((-1,) + (1,) * (len(dims) - dim - 1))

    level = one(*pieces[0])
    for cut in pieces[1:]:
        level = level * one(*cut)
    return level


def centred(key, dims, scale, limit, pieces=(), held_as=jnp.bfloat16):
    gain = shard_levels(key, dims, pieces, -0.22, 0.18) if pieces else 1.0
    entries = jax.random.normal(key, dims, jnp.float32) * scale * gain
    return jnp.minimum(jnp.maximum(entries, -limit), limit).astype(held_as)


def setup_inputs(seed: int = 0) -> dict:
    key_of = jax.random.split(jax.random.key(seed), 8)
    return {
        "source_points": centred(key_of[0], (3, POINTS), 1.0, 5.0, ((1, 8),), jnp.float32),
        "target_points": draw_target_points(jax.random.fold_in(key_of[7], 71), 0),
        "source_logw": centred(key_of[2], (POINTS,), 1.0, 4.0, ((0, 8),), jnp.float32),
        "target_logw": centred(key_of[3], (POINTS,), 1.0, 4.0, ((0, 8),), jnp.float32),
        "warm_start": draw_warm_start(jax.random.fold_in(key_of[7], 71), 0),
        "pairs": draw_pairs(jax.random.fold_in(key_of[7], 71), 0),
        "owner_slot": draw_owner_slot(jax.random.fold_in(key_of[7], 71), 0),
    }


EPSILON = 0.5
DUSTBIN = 0.0
VERY_LOW = -1.0e30


def cost_tile(source_block, target_block):
    first = source_block[0][:, None] - target_block[0][None, :]
    second = source_block[1][:, None] - target_block[1][None, :]
    third = source_block[2][:, None] - target_block[2][None, :]
    return first * first + second * second + third * third


def fold_block(carry_max, carry_sum, block_id, tile_max, tile_sum):
    old_max = carry_max[block_id]
    old_sum = carry_sum[block_id]
    new_max = jnp.maximum(old_max, tile_max)
    new_sum = old_sum * jnp.exp(old_max - new_max) + tile_sum * jnp.exp(tile_max - new_max)
    return carry_max.at[block_id].set(new_max), carry_sum.at[block_id].set(new_sum)


def finish(total_max, total_sum):
    shifted = jnp.maximum(total_max, DUSTBIN)
    return -EPSILON * (shifted + jnp.log(jnp.exp(DUSTBIN - shifted) + total_sum * jnp.exp(total_max - shifted)))


def reference(source_points, target_points, source_logw, target_logw, warm_start, pairs, owner_slot):
    block_count = N_BLK * NB_DEV
    src_ids = pairs[:, :, 0, :].reshape(-1)
    tgt_ids = pairs[:, :, 1, :].reshape(-1)
    live = tgt_ids >= 0
    src_block = jnp.where(live, src_ids, 0).astype(jnp.int32)
    tgt_block = owner_slot[jnp.where(live, tgt_ids, 0)].astype(jnp.int32)
    src_pts = source_points.reshape(3, block_count, BS)
    tgt_pts = target_points.reshape(3, block_count, BS)
    src_mass = source_logw.reshape(block_count, BS)
    tgt_mass = target_logw.reshape(block_count, BS)
    target_pot = warm_start.reshape(block_count, BS)
    start_max = jnp.full((block_count, BS), VERY_LOW, jnp.float32)
    start_sum = jnp.zeros((block_count, BS), jnp.float32)

    def row_half(target_now):
        def visit(carry, entry):
            s_id, t_id, alive = entry
            tile = cost_tile(src_pts[:, s_id], tgt_pts[:, t_id])
            term = tgt_mass[t_id][None, :] + (target_now[t_id][None, :] - tile) / EPSILON
            tile_max = jnp.max(term, axis=1)
            tile_sum = jnp.sum(jnp.exp(term - tile_max[:, None]), axis=1)
            tile_max = jnp.where(alive, tile_max, VERY_LOW)
            tile_sum = jnp.where(alive, tile_sum, 0.0)
            return fold_block(carry[0], carry[1], s_id, tile_max, tile_sum), None

        result, unused = lax.scan(visit, (start_max, start_sum), (src_block, tgt_block, live))
        return finish(result[0], result[1])

    def column_half(source_now):
        def visit(carry, entry):
            s_id, t_id, alive = entry
            tile = cost_tile(src_pts[:, s_id], tgt_pts[:, t_id])
            term = src_mass[s_id][:, None] + (source_now[s_id][:, None] - tile) / EPSILON
            tile_max = jnp.max(term, axis=0)
            tile_sum = jnp.sum(jnp.exp(term - tile_max[None, :]), axis=0)
            tile_max = jnp.where(alive, tile_max, VERY_LOW)
            tile_sum = jnp.where(alive, tile_sum, 0.0)
            return fold_block(carry[0], carry[1], t_id, tile_max, tile_sum), None

        result, unused = lax.scan(visit, (start_max, start_sum), (src_block, tgt_block, live))
        return finish(result[0], result[1])

    source_pot = start_sum
    for sweep in range(ITERS):
        source_pot = row_half(target_pot)
        target_pot = column_half(source_pot)
    return source_pot.reshape(-1), target_pot.reshape(-1)
```

```python
import functools

import jax
import jax.numpy as jnp
from jax import lax
from jax.experimental import pallas as pl
from jax.experimental.pallas import tpu as pltpu
from jax.sharding import PartitionSpec as P

BS = 256
ITERS = 2
GROUP_ROWS = 8
LOG2E = 1.4426950408889634
LN2 = 0.6931471805599453
EPSILON = 0.5
INV_EPS2 = LOG2E / EPSILON
LOW = -1e30
MESH = pl.DeviceIdType.MESH
F32 = jnp.float32


def log2(value):
    return jnp.log(value) * LOG2E


def split3(value):
    high = value.astype(jnp.bfloat16).astype(F32)
    rest = value - high
    middle = rest.astype(jnp.bfloat16).astype(F32)
    return high, middle, rest - middle


def tile_terms(rows, columns):
    r1, r2, r3 = split3(rows)
    c1, c2, c3 = split3(columns)
    left = jnp.concatenate((r1, r1, r2, r2, r1, r3), axis=0).astype(jnp.bfloat16)
    right = jnp.concatenate((c1, c2, c1, c2, c3, c1), axis=0).astype(jnp.bfloat16)
    return lax.dot_general(left, right, (((0,), (0,)), ((), ())), preferred_element_type=F32)


def lse_rows(terms):
    top = jnp.max(terms, axis=0, keepdims=True)
    return top + log2(jnp.sum(jnp.exp2(terms - top), axis=0, keepdims=True))


def wait_bytes(ref, sem):
    pltpu.make_async_copy(ref, ref, sem).wait()


def gather(hot, table):
    total = None
    for part in split3(table):
        one = jnp.dot(hot, part.astype(jnp.bfloat16), preferred_element_type=F32)
        total = one if total is None else total + one
    return total


def kernel(
    groups, side, capacity, nb,
    pairs_v, owner, src_pts, tgt_pts, src_mass, tgt_mass, warm,
    out_src, out_tgt,
    ids_send, ids_src, ids_tgt, hot_src, hot_tgt, pick_src, pick_tgt,
    got, src_pack, send_pack, recv_pack, mass_src, mass_tgt, bias_src, send_pot, recv_pot,
    terms, merged, send_col, recv_col, dense, stage1, stage2, full,
    ids_sem, pack_sem, pot_sem, col_sem, red_sem,
):
    b = lax.axis_index("blk")
    p = lax.axis_index("pair")
    z, y = p // side, p % side
    rows = groups * GROUP_ROWS
    seg = nb // 2 // side

    def blk_peer(d):
        return {"blk": lax.rem(b + d, groups)}

    def y_peer(d):
        return {"pair": z * side + lax.rem(y + d, side)}

    def z_peer(d):
        return {"pair": lax.rem(z + d, side) * side + y}

    barrier = pltpu.get_barrier_semaphore()

    def greet(peer, count):
        def one(d, carry):
            pl.semaphore_signal(barrier, inc=1, device_id=peer(d), device_id_type=MESH)
            return carry

        lax.fori_loop(1, count, one, 0)

    greet(blk_peer, groups)
    greet(y_peer, side)
    greet(z_peer, side)

    def send_all(peer, count, src_of, dst, sems):
        def one(d, carry):
            pltpu.make_async_remote_copy(
                src_ref=src_of(d), dst_ref=dst, send_sem=sems.at[0], recv_sem=sems.at[1],
                device_id=peer(d), device_id_type=MESH,
            ).start()
            return carry

        lax.fori_loop(1, count, one, 0)

    row = lax.broadcasted_iota(jnp.int32, (rows, 128), 0)
    lane = lax.broadcasted_iota(jnp.int32, (rows, 128), 1)
    group, member = row // GROUP_ROWS, row % GROUP_ROWS
    listed = member < capacity
    own_lane = jnp.where(listed, group * capacity + member, -1) == lane

    def column(values):
        return jnp.sum(jnp.where(own_lane, values.astype(F32), 0.0), axis=1, keepdims=True)

    source_id = jnp.broadcast_to(column(pairs_v[0:1, :]), (rows, 128)).astype(jnp.int32)
    target_id = jnp.broadcast_to(column(pairs_v[1:2, :]), (rows, 128)).astype(jnp.int32)
    live = listed & (target_id >= 0)
    ids_src[...] = jnp.where(live, source_id - b * nb, -1).reshape(groups, GROUP_ROWS, 128)
    table_rows = owner.shape[0]
    high = jnp.where(target_id[:, :table_rows] // 128 == lane[:, :table_rows], 1.0, 0.0)
    slot = gather(high.astype(jnp.bfloat16), owner[...].astype(F32))
    slot = jnp.sum(jnp.where(target_id % 128 == lane, slot, 0.0), axis=1, keepdims=True)
    slot = jnp.broadcast_to(slot, (rows, 128)).astype(jnp.int32)
    ids_send[...] = jnp.where(live, slot - group * nb, -1).reshape(groups, GROUP_ROWS, 128)

    pl.semaphore_wait(barrier, groups - 1 + 2 * (side - 1))
    send_all(blk_peer, groups, lambda d: ids_send.at[lax.rem(b + d, groups)], ids_tgt.at[b], ids_sem)
    ids_tgt[b] = ids_send[b]

    row8 = lax.broadcasted_iota(jnp.int32, (GROUP_ROWS, BS), 0)
    low_rows = jnp.full((groups, GROUP_ROWS, BS), LOW, F32)
    terms[...] = low_rows
    merged[...] = low_rows
    for it in range(ITERS):
        send_col[it] = low_rows

    def one_hots(ids, place, pick):
        ids = ids[...].reshape(rows, 128)
        if nb > 128:
            wide = jnp.concatenate([ids] * (nb // 128), axis=1)
        else:
            wide = ids[:, :nb]
        match = wide == lax.broadcasted_iota(jnp.int32, (rows, nb), 1)
        pick[...] = jnp.where(match, 1.0, 0.0).astype(jnp.bfloat16)
        lanes = jnp.sum(jnp.where(row == lane, ids.astype(F32), 0.0), axis=0, keepdims=True)
        again = jnp.where((ids.astype(F32) == lanes) & (row < lane), 1.0, 0.0)
        again = jnp.max(again, axis=0, keepdims=True)
        block = lax.broadcasted_iota(jnp.int32, (nb, 128), 0).astype(F32)
        lane_nb = lax.broadcasted_iota(jnp.int32, (nb, 128), 1)
        first = jnp.where((lane_nb < rows) & (again == 0.0) & (block == lanes), 1.0, 0.0)
        none = jnp.where(jnp.sum(first, axis=1, keepdims=True) > 0.0, 0.0, 1.0)
        place[...] = jnp.where(lane_nb == rows, none, first).astype(jnp.bfloat16)

    def make_pack(pack, places, ones):
        fixed = jnp.zeros((GROUP_ROWS, BS), F32)
        for r in ones:
            fixed = jnp.where(row8 == r, 1.0, fixed)

        def one_group(g, carry):
            for c in range(capacity):
                k = g * capacity + c
                pack[k] = fixed
                for i, r in enumerate(places):
                    pack[k, r : r + 1, :] = got[i, g, c : c + 1, :]
            return carry

        lax.fori_loop(0, groups, one_group, 0)

    def fetch_points(pick, points, scale):
        square = None
        for i in range(3):
            x = gather(pick[...], points[i])
            got[i] = (x * scale).reshape(groups, GROUP_ROWS, BS)
            square = x * x if square is None else square + x * x
        got[3] = (square * (-INV_EPS2)).reshape(groups, GROUP_ROWS, BS)

    shape3 = (groups, GROUP_ROWS, BS)
    one_hots(ids_src, hot_src, pick_src)
    fetch_points(pick_src, src_pts, 2.0 * INV_EPS2)
    make_pack(src_pack, (0, 1, 2, 4), (3, 5))
    mass_src[...] = (gather(pick_src[...], src_mass[...]) * LOG2E).reshape(shape3)

    wait_bytes(ids_tgt.at[pl.ds(0, groups - 1)], ids_sem.at[1])
    one_hots(ids_tgt, hot_tgt, pick_tgt)
    fetch_points(pick_tgt, tgt_pts, 1.0)
    mass = gather(pick_tgt[...], tgt_mass[...]) * LOG2E
    mass_tgt[...] = mass.reshape(shape3)
    got[4] = (mass + gather(pick_tgt[...], warm[...]) * INV_EPS2).reshape(shape3)
    make_pack(send_pack, (0, 1, 2, 3, 5), (4,))

    def block_of(g):
        return pl.ds(g * capacity, capacity)

    send_all(
        blk_peer, groups, lambda d: send_pack.at[block_of(lax.rem(b + d, groups))],
        recv_pack.at[block_of(b)], pack_sem,
    )
    for c in range(capacity):
        recv_pack[b * capacity + c] = send_pack[b * capacity + c]
    wait_bytes(recv_pack.at[pl.ds(0, (groups - 1) * capacity)], pack_sem.at[1])

    def merge_and_place(ids, values, hot, target):
        def one_group(g, carry):
            for c in range(capacity):
                same = ids[...].reshape(rows, 128) == ids[g, c : c + 1, :]
                for h in range(BS // 128):
                    part = values[:, :, 128 * h : 128 * (h + 1)].reshape(rows, 128)
                    picked = jnp.where(same, part, LOW)
                    merged[g, c : c + 1, 128 * h : 128 * (h + 1)] = lse_rows(picked)
            return carry

        lax.fori_loop(0, groups, one_group, 0)
        one, two, three = split3(merged[...].reshape(rows, BS))
        last = 128 - rows
        none = jnp.full((last, BS), LOW, F32)
        zero = jnp.zeros((last, BS), F32)
        first = jnp.concatenate((one, none), axis=0).astype(jnp.bfloat16)
        total = jnp.dot(hot[...], first, preferred_element_type=F32)
        for part in (two, three):
            more = jnp.concatenate((part, zero), axis=0).astype(jnp.bfloat16)
            total = total + jnp.dot(hot[...], more, preferred_element_type=F32)
        target[...] = total

    def reduce_pairs(a):
        places = (y, z)
        firsts = (y_peer, z_peer)
        seconds = (z_peer, y_peer)
        for h in range(2):
            mine = places[h]

            def chunk(d, h=h, mine=mine):
                first = h * (nb // 2) + lax.rem(mine + d, side) * seg
                return dense.at[a, pl.ds(pl.multiple_of(first, seg), seg)]

            send_all(firsts[h], side, chunk, stage1.at[a, h, mine], red_sem.at[a, h, 0])
            own = pl.multiple_of(h * (nb // 2) + mine * seg, seg)
            stage1[a, h, mine] = dense[a, pl.ds(own, seg), :]
        for h in range(2):
            wait_bytes(stage1.at[a, h, pl.ds(0, side - 1)], red_sem.at[a, h, 0, 1])
            arrived = stage1[a, h]
            top = jnp.max(arrived, axis=0)
            part = top + log2(jnp.sum(jnp.exp2(arrived - top[None]), axis=0))
            other = places[1 - h]
            stage2[a, h, other] = part
            send_all(
                seconds[h], side, lambda d, h=h, other=other: stage2.at[a, h, other],
                stage2.at[a, h, other], red_sem.at[a, h, 1],
            )
        for h in range(2):
            mine = places[h]
            wait_bytes(stage2.at[a, h, pl.ds(0, side - 1)], red_sem.at[a, h, 1, 1])
            arrived = stage2[a, h]
            top = jnp.maximum(jnp.max(arrived, axis=0), 0.0)
            total = jnp.exp2(-top) + jnp.sum(jnp.exp2(arrived - top[None]), axis=0)
            own = pl.multiple_of(h * (nb // 2) + mine * seg, seg)
            full[a, pl.ds(own, seg), :] = top + log2(total)
            place = full.at[a, pl.ds(own, seg)]
            send_all(firsts[h], side, lambda d, place=place: place, place, red_sem.at[a, h, 2])
        for h in range(2):
            wait_bytes(full.at[a, pl.ds(0, (side - 1) * seg)], red_sem.at[a, h, 2, 1])

    for it in range(ITERS):
        if it > 0:
            pot = gather(pick_tgt[...], full[2 * it - 1])
            send_pot[...] = mass_tgt[...] - pot.reshape(shape3)
            send_all(
                blk_peer, groups, lambda d: send_pot.at[lax.rem(b + d, groups)],
                recv_pot.at[b], pot_sem,
            )
            recv_pot[b] = send_pot[b]
            wait_bytes(recv_pot.at[pl.ds(0, groups - 1)], pot_sem.at[1])

        def row_group(g, carry, it=it):
            for c in range(capacity):
                k = g * capacity + c
                target = recv_pack[k]
                if it > 0:
                    target = jnp.where(row8 == 5, recv_pot[g, c : c + 1, :], target)
                terms[g, c : c + 1, :] = lse_rows(tile_terms(target, src_pack[k]))
            return carry

        lax.fori_loop(0, groups, row_group, 0)
        merge_and_place(ids_src, terms, hot_src, dense.at[2 * it])
        reduce_pairs(2 * it)

        bias_src[...] = mass_src[...] - gather(pick_src[...], full[2 * it]).reshape(shape3)

        def column_group(g, carry, it=it):
            for c in range(capacity):
                k = g * capacity + c
                source = jnp.where(row8 == 5, bias_src[g, c : c + 1, :], src_pack[k])
                target = jnp.where(row8 == 5, 1.0, recv_pack[k])
                send_col[it, g, c : c + 1, :] = lse_rows(tile_terms(source, target))
            return carry

        lax.fori_loop(0, groups, column_group, 0)
        send_all(
            blk_peer, groups, lambda d, it=it: send_col.at[it, lax.rem(b + d, groups)],
            recv_col.at[it, b], col_sem.at[it],
        )
        recv_col[it, b] = send_col[it, b]
        wait_bytes(recv_col.at[it, pl.ds(0, groups - 1)], col_sem.at[it, 1])
        terms[...] = recv_col[it]
        merge_and_place(ids_tgt, terms, hot_tgt, dense.at[2 * it + 1])
        reduce_pairs(2 * it + 1)

    out_src[...] = full[2 * ITERS - 2] * (-EPSILON * LN2)
    out_tgt[...] = full[2 * ITERS - 1] * (-EPSILON * LN2)

    def drain(sem, ref, count):
        def one(d, carry):
            wait_bytes(ref, sem)
            return carry

        lax.fori_loop(1, count, one, 0)

    drain(ids_sem.at[0], ids_send.at[0], groups)
    drain(pack_sem.at[0], send_pack.at[pl.ds(0, capacity)], groups)
    if ITERS > 1:
        drain(pot_sem.at[0], send_pot.at[0], groups)
    for it in range(ITERS):
        drain(col_sem.at[it, 0], send_col.at[it, 0], groups)
    for a in range(2 * ITERS):
        for h in range(2):
            for stage in range(3):
                drain(red_sem.at[a, h, stage, 0], dense.at[a, pl.ds(0, seg)], side)


def per_device(
    source_points, target_points, source_logw, target_logw, warm_start, pairs, owner_slot
):
    groups = lax.axis_size("blk")
    side = round(lax.axis_size("pair") ** 0.5)
    points = source_logw.shape[0]
    nb = points // BS
    capacity = pairs.shape[-1] // groups
    entries = groups * capacity
    rows = groups * GROUP_ROWS
    seg = nb // 2 // side
    reductions = 2 * ITERS
    pairs = pairs[0, 0]
    padded = jnp.pad(pairs, ((0, 6), (0, 128 - entries)), constant_values=-1)
    slots = -(-owner_slot.shape[0] // 2048) * 2048
    owner = jnp.pad(owner_slot, (0, slots - owner_slot.shape[0])).reshape(-1, 128)
    vmem = pl.BlockSpec(memory_space=pltpu.VMEM)
    out = jax.ShapeDtypeStruct((nb, BS), F32)
    dma = pltpu.SemaphoreType.DMA
    source_pot, target_pot = pl.pallas_call(
        functools.partial(kernel, groups, side, capacity, nb),
        out_shape=(out, out),
        in_specs=[vmem] * 7,
        out_specs=(vmem, vmem),
        scratch_shapes=[
            *[pltpu.VMEM((groups, GROUP_ROWS, 128), jnp.int32)] * 3,
            *[pltpu.VMEM((nb, 128), jnp.bfloat16)] * 2,
            *[pltpu.VMEM((rows, nb), jnp.bfloat16)] * 2,
            pltpu.VMEM((5, groups, GROUP_ROWS, BS), F32),
            *[pltpu.VMEM((entries, GROUP_ROWS, BS), F32)] * 3,
            *[pltpu.VMEM((groups, GROUP_ROWS, BS), F32)] * 7,
            *[pltpu.VMEM((ITERS, groups, GROUP_ROWS, BS), F32)] * 2,
            pltpu.VMEM((reductions, nb, BS), F32),
            *[pltpu.VMEM((reductions, 2, side, seg, BS), F32)] * 2,
            pltpu.VMEM((reductions, nb, BS), F32),
            dma((2,)),
            dma((2,)),
            dma((2,)),
            dma((ITERS, 2)),
            dma((reductions, 2, 3, 2)),
        ],
        compiler_params=pltpu.CompilerParams(
            collective_id=0, has_side_effects=True, vmem_limit_bytes=40 * 1024 * 1024
        ),
        name="sinkhorn",
    )(
        padded, owner,
        source_points.reshape(3, nb, BS), target_points.reshape(3, nb, BS),
        source_logw.reshape(nb, BS), target_logw.reshape(nb, BS), warm_start.reshape(nb, BS),
    )
    return source_pot.reshape(-1), target_pot.reshape(-1)


def solution(mesh):
    return jax.shard_map(
        per_device,
        mesh=mesh,
        in_specs=(
            P(None, "blk"),
            P(None, "blk"),
            P("blk"),
            P("blk"),
            P("blk"),
            P("blk", "pair", None, None),
            P(),
        ),
        out_specs=(P("blk"), P("blk")),
        check_vma=False,
    )
```

```python
import functools

import jax
import jax.numpy as jnp
from jax import lax
from jax.experimental import pallas as pl
from jax.experimental.pallas import tpu as pltpu
from jax.sharding import PartitionSpec as P

BS = 256
HALF = 128
ITERS = 2
GROUP_ROWS = 8
LOG2E = 1.4426950408889634
LN2 = 0.6931471805599453
EPSILON = 0.5
INV_EPS2 = LOG2E / EPSILON
LOW = -1e30
MESH = pl.DeviceIdType.MESH
F32 = jnp.float32
BF16 = jnp.bfloat16


def log2(value):
    return jnp.log(value) * LOG2E


def split3(value):
    high = value.astype(BF16).astype(F32)
    rest = value - high
    middle = rest.astype(BF16).astype(F32)
    return high, middle, rest - middle


def left_parts(value):
    one, two, three = split3(value)
    return jnp.concatenate((one, one, two, two, one, three), axis=0).astype(BF16)


def right_parts(value):
    one, two, three = split3(value)
    return jnp.concatenate((one, two, one, two, three, one), axis=0).astype(BF16)


def tile_lse(left, right):
    terms = lax.dot_general(left, right, (((0,), (0,)), ((), ())), preferred_element_type=F32)
    top = jnp.max(terms, axis=0, keepdims=True)
    return top + log2(jnp.sum(jnp.exp2(terms - top), axis=0, keepdims=True))


def lse_pair(first, second):
    top = jnp.maximum(first, second)
    return top + log2(jnp.exp2(first - top) + jnp.exp2(second - top))


def tile_all(lefts, rights):
    return [tile_lse(one, two) for one, two in zip(lefts, rights)]


def gather(hot, parts):
    total = None
    for part in parts:
        one = jnp.dot(hot, part.astype(BF16), preferred_element_type=F32)
        total = one if total is None else total + one
    return total


def lanes_of(h):
    return slice(h * HALF, (h + 1) * HALF)


def wait_bytes(ref, sem):
    pltpu.make_async_copy(ref, ref, sem).wait()


def far_first(k, size):
    return size // 2 + (1 - 2 * (k % 2)) * ((k + 1) // 2)


def kernel(
    groups, side, capacity, nb,
    pairs_v, owner, src_pts, tgt_pts, src_mass, tgt_mass, warm,
    out_src, out_tgt,
    ids_send, ids_src, ids_tgt, own_ids, lists, place, pick, pick_src, pick_tgt, table,
    got_src, got_send, got_recv, src_pack, tgt_pack, left, right_src, right_tgt,
    mass_src, mass_tgt, bias, send_pot, recv_pot, terms, partial, values_c, merged, send_col, recv_col,
    spread, spread_got, placed, row_sum, asked, asked_got, dense, stage1, stage2, full,
    ids_sem, list_sem, pack_sent, pack_sem, pot_sent, pot_sem, col_sem, spread_sem, red_sem,
):
    b = lax.axis_index("blk")
    p = lax.axis_index("pair")
    z, y = p // side, p % side
    rows = groups * GROUP_ROWS
    seg = nb // side
    chips = groups // 2

    def blk_index(k):
        x = lax.rem(b // 2 + far_first(k // 2, chips), chips)
        return x * 2 + lax.rem(b + 1 + k, 2)

    def near(k):
        return blk_index(groups - 1 - k)

    def y_index(k):
        return z * side + lax.rem(y + far_first(k, side), side)

    def z_index(k):
        return lax.rem(z + far_first(k, side), side) * side + y

    barrier = pltpu.get_barrier_semaphore()

    def greet(axis, index, count):
        def one(k, carry):
            pl.semaphore_signal(barrier, inc=1, device_id={axis: index(k)}, device_id_type=MESH)
            return carry

        lax.fori_loop(0, count - 1, one, 0)

    greet("blk", blk_index, groups)
    greet("pair", y_index, side)
    greet("pair", z_index, side)

    def send(axis, peer, src, dst, sent, arrived):
        pltpu.make_async_remote_copy(
            src_ref=src, dst_ref=dst, send_sem=sent, recv_sem=arrived,
            device_id={axis: peer}, device_id_type=MESH,
        ).start()

    entries = groups * capacity
    row = lax.broadcasted_iota(jnp.int32, (rows, HALF), 0)
    lane = lax.broadcasted_iota(jnp.int32, (rows, HALF), 1)
    group, member = row // GROUP_ROWS, row % GROUP_ROWS
    listed = member < capacity
    own_lane = jnp.where(listed, group * capacity + member, -1)[:, :entries] == lane[:, :entries]

    def column(values):
        picked = jnp.where(own_lane, values.astype(F32), 0.0)
        total = jnp.sum(picked, axis=1, keepdims=True)
        return jnp.broadcast_to(total, (rows, HALF)).astype(jnp.int32)

    shape_ids = (groups, GROUP_ROWS, HALF)
    source_id = column(pairs_v[0:1, :])
    target_id = column(pairs_v[1:2, :])
    live = listed & (target_id >= 0)
    ids_src[...] = jnp.where(live, source_id - b * nb, -1).reshape(shape_ids)
    table_rows = owner.shape[0]
    high = jnp.where(target_id[:, :table_rows] // HALF == lane[:, :table_rows], 1.0, 0.0)
    slot = gather(high.astype(BF16), split3(owner[...].astype(F32)))
    slot = jnp.sum(jnp.where(target_id % HALF == lane, slot, 0.0), axis=1, keepdims=True)
    slot = jnp.broadcast_to(slot, (rows, HALF)).astype(jnp.int32)
    ids_send[...] = jnp.where(live, slot - group * nb, -1).reshape(shape_ids)

    pl.semaphore_wait(barrier, groups - 1 + 2 * (side - 1))

    def send_ids(k, carry):
        g = blk_index(k)
        send("blk", g, ids_send.at[g], ids_tgt.at[b], ids_sem.at[0], ids_sem.at[1])
        return carry

    lax.fori_loop(0, groups - 1, send_ids, 0)
    ids_tgt[b] = ids_send[b]

    def vector_half(ref, h):
        return ref[pl.ds(h, nb, stride=2), :]

    def pick_matrix(ids, pick):
        ids = ids[...].reshape(rows, HALF)
        wide = jnp.concatenate([ids] * (nb // HALF), axis=1) if nb > HALF else ids[:, :nb]
        match = wide == lax.broadcasted_iota(jnp.int32, (rows, nb), 1)
        pick[...] = jnp.where(match, 1.0, 0.0).astype(BF16)

    lane_row = lane % entries
    lane_place = (lane_row % groups) * GROUP_ROWS + lane_row // groups

    def make_list(ids):
        ids = ids[...].reshape(rows, HALF).astype(F32)
        inside = lane < 3 * entries
        lanes = jnp.sum(jnp.where((row == lane_place) & inside, ids, 0.0), axis=0, keepdims=True)
        before = listed & (member * groups + group < lane_row)
        again = jnp.max(jnp.where((ids == lanes) & before, 1.0, 0.0), axis=0, keepdims=True)
        once = jnp.where((again > 0.0) | jnp.logical_not(inside[0:1, :]), -1.0, lanes)
        line = lax.broadcasted_iota(jnp.int32, (GROUP_ROWS, HALF), 0)
        return jnp.where(line == 0, lanes, jnp.where(line == 1, once, -1.0)).astype(jnp.int32)

    def send_list(s):
        for axis, (index, mine) in enumerate(((y_index, y), (z_index, z))):
            spot = lists.at[s, axis, mine]

            def one(k, carry, index=index, spot=spot, axis=axis):
                sems = list_sem.at[s, axis]
                send("pair", index(k), spot, spot, sems.at[0], sems.at[1])
                return carry

            lax.fori_loop(0, side - 1, one, 0)

    def read_lists(s):
        block = lax.broadcasted_iota(jnp.int32, (nb, HALF), 0)
        lane_nb = lax.broadcasted_iota(jnp.int32, (nb, HALF), 1)
        ones = jnp.ones((HALF, HALF), BF16)
        row_e = lax.broadcasted_iota(jnp.int32, (entries, HALF), 0)
        lane_e = lax.broadcasted_iota(jnp.int32, (entries, HALF), 1)
        for axis in range(2):
            wait_bytes(lists.at[s, axis, pl.ds(0, side - 1)], list_sem.at[s, axis, 1])

            def one(i, carry, axis=axis):
                match = jnp.where(block == lists[s, axis, i, 1:2, :], 1.0, 0.0)
                count = jnp.dot(match.astype(BF16), ones, preferred_element_type=F32)
                none = jnp.where(count > 0.5, 0.0, 1.0)
                place[s, axis, i] = jnp.where(lane_nb == 3 * entries, none, match).astype(BF16)
                return carry

            lax.fori_loop(0, side, one, 0)
            columns = []
            for i in range(side):
                ids = jnp.where(row_e == lane_e, lists[s, axis, i, 0:1, :], 0).astype(F32)
                ids = jnp.sum(ids, axis=1, keepdims=True)
                columns.append(jnp.broadcast_to(ids, (entries, HALF)).astype(jnp.int32))
            ids = jnp.concatenate(columns, axis=0)
            wide = jnp.concatenate([ids] * (nb // HALF), axis=1) if nb > HALF else ids[:, :nb]
            match = wide == lax.broadcasted_iota(jnp.int32, (side * entries, nb), 1)
            pick[s, axis] = jnp.where(match, 1.0, 0.0).astype(BF16)

    def to_compact(ref, target):
        for c in range(capacity):
            for g in range(groups):
                target[c, g : g + 1, :] = ref[g, c : c + 1, :]

    def to_wide(values, target):
        for c in range(capacity):
            for g in range(groups):
                target[g, c : c + 1, :] = values[c, g : g + 1, :]

    row8 = lax.broadcasted_iota(jnp.int32, (GROUP_ROWS, BS), 0)
    row8_half = lax.broadcasted_iota(jnp.int32, (GROUP_ROWS, HALF), 0)

    def pack_rows(points, scale, flipped, bias_row):
        square = points[0] * points[0] + points[1] * points[1] + points[2] * points[2]
        norm = square * (-INV_EPS2)
        lines = [point * scale for point in points]
        lines += [1.0, norm] if flipped else [norm, 1.0]
        lines.append(bias_row)
        packed = jnp.zeros((GROUP_ROWS, BS), F32)
        for r, line in enumerate(lines):
            packed = jnp.where(row8 == r, line, packed)
        return packed

    def own_list(s, ids):
        tile = make_list(ids)
        lists[s, 0, y] = tile
        lists[s, 1, z] = tile
        send_list(s)
        to_compact(ids, own_ids.at[s])

    for i in range(3):
        for j, part in enumerate(split3(tgt_pts[i])):
            table[i, j] = part.astype(BF16)
    for h in range(2):
        first = vector_half(tgt_mass, h) * LOG2E + vector_half(warm, h) * INV_EPS2
        for j, part in enumerate(split3(first)):
            table[3, j, :, lanes_of(h)] = part.astype(BF16)
    low_half = jnp.full(shape_ids, LOW, F32)
    for h in range(2):
        terms[h] = low_half
        partial[h] = low_half
        send_pot[h] = low_half
    shape3 = (groups, GROUP_ROWS, BS)
    own_list(0, ids_src)
    pick_matrix(ids_src, pick_src)
    for i in range(3):
        got_src[i] = gather(pick_src[...], split3(src_pts[i])).reshape(shape3)

    wait_bytes(ids_tgt.at[pl.ds(0, groups - 1)], ids_sem.at[1])
    pick_matrix(ids_tgt, pick_tgt)
    for i in range(4):
        found = gather(pick_tgt[...], [table[i, j] for j in range(3)]).reshape(shape3)
        for g in range(groups):
            got_send[g, i] = found[g]

    def send_pack(k, carry):
        g = blk_index(k)
        send("blk", g, got_send.at[g], got_recv.at[b], pack_sent, pack_sem.at[b])
        return carry

    lax.fori_loop(0, groups - 1, send_pack, 0)
    got_recv[b] = got_send[b]

    def source_group(g, carry):
        for c in range(capacity):
            k = g * capacity + c
            points = [got_src[i, g, c : c + 1, :] for i in range(3)]
            packed = pack_rows(points, 2.0 * INV_EPS2, True, 1.0)
            src_pack[k] = packed
            right_src[k] = right_parts(packed)
        return carry

    lax.fori_loop(0, groups, source_group, 0)
    own_list(1, ids_tgt)
    for h in range(2):
        found = gather(pick_src[...], split3(vector_half(src_mass, h) * LOG2E))
        mass_src[h] = found.reshape(shape_ids)
        found = gather(pick_tgt[...], split3(vector_half(tgt_mass, h) * LOG2E))
        mass_tgt[h] = found.reshape(shape_ids)

    def merge(s, values, target):
        to_compact(values, values_c)

        def one(c, carry):
            for g in range(groups):
                same = own_ids[s].reshape(entries, HALF) == own_ids[s, c, g : g + 1, :]
                picked = jnp.where(same, values_c[...].reshape(entries, HALF), LOW)
                top = jnp.max(picked, axis=0, keepdims=True)
                total = jnp.sum(jnp.exp2(picked - top), axis=0, keepdims=True)
                target[c, g : g + 1, :] = top + log2(total)
            return carry

        lax.fori_loop(0, capacity, one, 0)

    def put(matrix, values):
        one, two, three = split3(values.reshape(entries, HALF))
        none = jnp.full((HALF - 3 * entries, HALF), LOW, F32)
        parts = jnp.concatenate((one, two, three, none), axis=0).astype(BF16)
        return jnp.dot(matrix, parts, preferred_element_type=F32)

    places = (y, z)
    firsts = (y_index, z_index)
    seconds = (z_index, y_index)

    def coordinate(h, peer):
        return lax.rem(peer, side) if h == 0 else peer // side

    def spread_start(a, h):
        mine = places[h]
        sems = spread_sem.at[a, h, 0]

        def one(k, carry):
            send("pair", firsts[h](k), spread.at[a, h], spread_got.at[a, h, mine], sems.at[0], sems.at[1])
            return carry

        lax.fori_loop(0, side - 1, one, 0)
        spread_got[a, h, mine] = spread[a, h]

    def spread_second(a, h, s):
        wait_bytes(spread_got.at[a, h, pl.ds(0, side - 1)], spread_sem.at[a, h, 0, 1])
        for i in range(side):
            placed[i] = put(place[s, h, i], spread_got[a, h, i])
        step = min(nb, 64)
        for q in range(nb // step):
            arrived = placed[:, q * step : (q + 1) * step, :]
            top = jnp.max(arrived, axis=0)
            total = jnp.sum(jnp.exp2(arrived - top[None]), axis=0)
            row_sum[h, q * step : (q + 1) * step, :] = top + log2(total)
        found = gather(pick[s, 1 - h], split3(row_sum[h]))
        asked[a, h] = found.reshape(side, capacity, groups, HALF)
        other = places[1 - h]
        sems = spread_sem.at[a, h, 1]

        def one(k, carry):
            peer = seconds[h](k)
            spot = asked.at[a, h, coordinate(1 - h, peer)]
            send("pair", peer, spot, asked_got.at[a, h, other], sems.at[0], sems.at[1])
            return carry

        lax.fori_loop(0, side - 1, one, 0)
        asked_got[a, h, other] = asked[a, h, other]

    def spread_end(a, h):
        wait_bytes(asked_got.at[a, h, pl.ds(0, side - 1)], spread_sem.at[a, h, 1, 1])
        arrived = asked_got[a, h]
        top = jnp.maximum(jnp.max(arrived, axis=0), 0.0)
        total = jnp.exp2(-top) + jnp.sum(jnp.exp2(arrived - top[None]), axis=0)
        return top + log2(total)

    def own_chunk(h):
        return pl.ds(pl.multiple_of(places[h] * seg, seg), seg)

    def reduce_start(h):
        mine = places[h]

        def one(k, carry):
            peer = firsts[h](k)
            chunk = pl.ds(pl.multiple_of(coordinate(h, peer) * seg, seg), seg)
            sems = red_sem.at[1, h, 0]
            send("pair", peer, dense.at[h, chunk], stage1.at[h, mine], sems.at[0], sems.at[1])
            return carry

        lax.fori_loop(0, side - 1, one, 0)
        stage1[h, mine] = dense[h, own_chunk(h), :]

    def reduce_second(o, h):
        other = places[1 - h]
        if o == 0:
            stage2[o, h, other] = row_sum[h, own_chunk(h), :]
        else:
            wait_bytes(stage1.at[h, pl.ds(0, side - 1)], red_sem.at[o, h, 0, 1])
            arrived = stage1[h]
            top = jnp.max(arrived, axis=0)
            stage2[o, h, other] = top + log2(jnp.sum(jnp.exp2(arrived - top[None]), axis=0))
        sems = red_sem.at[o, h, 1]

        def one(k, carry):
            spot = stage2.at[o, h, other]
            send("pair", seconds[h](k), spot, spot, sems.at[0], sems.at[1])
            return carry

        lax.fori_loop(0, side - 1, one, 0)

    def reduce_third(o, h):
        wait_bytes(stage2.at[o, h, pl.ds(0, side - 1)], red_sem.at[o, h, 1, 1])
        arrived = stage2[o, h]
        top = jnp.maximum(jnp.max(arrived, axis=0), 0.0)
        total = jnp.exp2(-top) + jnp.sum(jnp.exp2(arrived - top[None]), axis=0)
        full[o, h, own_chunk(h), :] = top + log2(total)
        sems = red_sem.at[o, h, 2]

        def one(k, carry):
            spot = full.at[o, h, own_chunk(h)]
            send("pair", firsts[h](k), spot, spot, sems.at[0], sems.at[1])
            return carry

        lax.fori_loop(0, side - 1, one, 0)

    def reduce_end(o, h, out):
        wait_bytes(full.at[o, h, pl.ds(0, (side - 1) * seg)], red_sem.at[o, h, 2, 1])
        out[pl.ds(h, nb, stride=2), :] = full[o, h] * (-EPSILON * LN2)

    def entries_of(gs):
        return [(g, c, g * capacity + c) for g in gs for c in range(capacity)]

    def by_pairs(step, order):
        def one(i, carry):
            step([order(2 * i), order(2 * i + 1)])
            return carry

        lax.fori_loop(0, groups // 2, one, 0)

    def as_they_come(step, ref, sem):
        wait_bytes(ref.at[near(1)], sem.at[near(1)])
        step([near(0), near(1)])

        def one(i, carry):
            gs = [near(2 * i), near(2 * i + 1)]
            for g in gs:
                wait_bytes(ref.at[g], sem.at[g])
            step(gs)
            return carry

        lax.fori_loop(1, groups // 2, one, 0)

    def store_rows(ref, where, totals):
        for (g, c, k), total in zip(where, totals):
            ref[g, c : c + 1, :] = total

    def first_rows(gs):
        where = entries_of(gs)
        packs = []
        for g, c, k in where:
            points = [got_recv[g, i, c : c + 1, :] for i in range(3)]
            packs.append(pack_rows(points, 1.0, False, got_recv[g, 3, c : c + 1, :]))
        lefts = [left_parts(packed) for packed in packs]
        totals = tile_all(lefts, [right_src[k, :, lanes_of(0)] for g, c, k in where])
        for (g, c, k), packed, here in zip(where, packs, lefts):
            tgt_pack[k] = packed
            left[k] = here
        store_rows(terms.at[0], where, totals)

    def second_rows(gs):
        where = entries_of(gs)
        lefts = [left[k] for g, c, k in where]
        store_rows(terms.at[1], where, tile_all(lefts, [right_src[k, :, lanes_of(1)] for g, c, k in where]))

    def row_lefts(h, where):
        return [
            left_parts(
                jnp.where(row8_half == 5, recv_pot[h, g, c : c + 1, :], tgt_pack[k, :, lanes_of(h)])
            )
            for g, c, k in where
        ]

    def store_halves(where, totals):
        for out in range(2):
            store_rows(partial.at[out], where, [total[:, lanes_of(out)] for total in totals])

    def early_rows(gs):
        where = entries_of(gs)
        store_halves(where, tile_all(row_lefts(0, where), [right_src[k] for g, c, k in where]))

    def late_rows(gs):
        where = entries_of(gs)
        lefts = row_lefts(1, where)
        totals = tile_all(lefts, [right_src[k, :, lanes_of(0)] for g, c, k in where])
        for (g, c, k), here in zip(where, lefts):
            left[k, :, lanes_of(1)] = here
        store_rows(terms.at[0], where, totals)

    def last_rows(gs):
        where = entries_of(gs)
        lefts = [left[k, :, lanes_of(1)] for g, c, k in where]
        store_rows(terms.at[1], where, tile_all(lefts, [right_src[k, :, lanes_of(1)] for g, c, k in where]))

    def column_lefts(h, where):
        return [
            left_parts(
                jnp.where(row8_half == 5, bias[h, g, c : c + 1, :], src_pack[k, :, lanes_of(h)])
            )
            for g, c, k in where
        ]

    def early_columns(gs):
        where = entries_of(gs)
        store_halves(where, tile_all(column_lefts(0, where), [right_tgt[k] for g, c, k in where]))

    def late_columns(it, out, gs):
        where = entries_of(gs)
        if out == 0:
            lefts = column_lefts(1, where)
        else:
            lefts = [left[k, :, lanes_of(1)] for g, c, k in where]
        totals = tile_all(lefts, [right_tgt[k, :, lanes_of(out)] for g, c, k in where])
        if out == 0:
            for (g, c, k), here in zip(where, lefts):
                left[k, :, lanes_of(1)] = here
        store_rows(terms.at[out], where, totals)
        for g in gs:
            send_col[it, out, g] = lse_pair(partial[out, g], terms[out, g])

    def target_group(gs):
        for g, c, k in entries_of(gs):
            right_tgt[k] = right_parts(jnp.where(row8 == 5, 1.0, tgt_pack[k]))

    for it in range(ITERS):
        a_src, a_tgt = 2 * it, 2 * it + 1
        last = it == ITERS - 1
        if it == 0:
            as_they_come(first_rows, got_recv, pack_sem)
        else:
            for h in range(2):
                to_wide(spread_end(a_src - 1, h), send_pot.at[h])
                send_pot[h] = mass_tgt[h] - send_pot[h]

                def pot_send(k, carry, h=h):
                    g = blk_index(k)
                    send("blk", g, send_pot.at[h, g], recv_pot.at[h, b], pot_sent.at[h], pot_sem.at[h, b])
                    return carry

                lax.fori_loop(0, groups - 1, pot_send, 0)
                recv_pot[h, b] = send_pot[h, b]
            as_they_come(early_rows, recv_pot.at[0], pot_sem.at[0])
            as_they_come(late_rows, recv_pot.at[1], pot_sem.at[1])
            terms[0] = lse_pair(partial[0], terms[0])
        merge(0, terms.at[0], spread.at[a_src, 0])
        spread_start(a_src, 0)
        by_pairs(second_rows if it == 0 else last_rows, near)
        if it > 0:
            terms[1] = lse_pair(partial[1], terms[1])
        merge(0, terms.at[1], spread.at[a_src, 1])
        spread_start(a_src, 1)
        if it == 0:
            read_lists(0)
        for h in range(2):
            spread_second(a_src, h, 0)
        if last:
            for h in range(2):
                reduce_second(0, h)
        if it == 0:
            by_pairs(target_group, near)
            read_lists(1)
        for h in range(2):
            to_wide(spread_end(a_src, h), bias.at[h])
            bias[h] = mass_src[h] - bias[h]
            if h == 0:
                by_pairs(early_columns, near)
        for out in range(2):
            def send_columns(gs, out=out, it=it):
                late_columns(it, out, gs)
                sems = col_sem.at[it, out]
                for g in gs:
                    send(
                        "blk", g, send_col.at[it, out, g], recv_col.at[it, out, b],
                        sems.at[0], sems.at[1],
                    )

            def far_pair(i, carry, send_columns=send_columns):
                send_columns([blk_index(2 * i), blk_index(2 * i + 1)])
                return carry

            lax.fori_loop(0, groups // 2 - 1, far_pair, 0)
            late_columns(it, out, [near(1), b])
            sems = col_sem.at[it, out]
            send(
                "blk", near(1), send_col.at[it, out, near(1)], recv_col.at[it, out, b],
                sems.at[0], sems.at[1],
            )
            recv_col[it, out, b] = send_col[it, out, b]
        if last:
            for h in range(2):
                reduce_third(0, h)
        for out in range(2):
            wait_bytes(recv_col.at[it, out, pl.ds(0, groups - 1)], col_sem.at[it, out, 1])
            if last:
                merge(1, recv_col.at[it, out], merged)
                dense[out] = put(place[1, 0, y], merged[...])
                reduce_start(out)
            else:
                merge(1, recv_col.at[it, out], spread.at[a_tgt, out])
                spread_start(a_tgt, out)
        if not last:
            for h in range(2):
                spread_second(a_tgt, h, 1)

    for h in range(2):
        reduce_end(0, h, out_src)
    for step in (reduce_second, reduce_third):
        for h in range(2):
            step(1, h)
    for h in range(2):
        reduce_end(1, h, out_tgt)

    def drain(sem, ref, count):
        def one(k, carry):
            wait_bytes(ref, sem)
            return carry

        lax.fori_loop(1, count, one, 0)

    drain(ids_sem.at[0], ids_send.at[0], groups)
    drain(pack_sent, got_send.at[0], groups)
    for h in range(2):
        if ITERS > 1:
            drain(pot_sent.at[h], send_pot.at[h, 0], groups)
        for it in range(ITERS):
            drain(col_sem.at[it, h, 0], send_col.at[it, h, 0], groups)
        for a in range(2 * ITERS - 1):
            for stage in range(2):
                drain(spread_sem.at[a, h, stage, 0], spread.at[a, h], side)
        for o in range(2):
            for stage in range(1 - o, 3):
                drain(red_sem.at[o, h, stage, 0], dense.at[h, pl.ds(0, seg)], side)
        for s in range(2):
            drain(list_sem.at[s, h, 0], lists.at[s, h, 0], side)


def per_device(
    source_points, target_points, source_logw, target_logw, warm_start, pairs, owner_slot
):
    groups = lax.axis_size("blk")
    side = round(lax.axis_size("pair") ** 0.5)
    points = source_logw.shape[0]
    nb = points // BS
    capacity = pairs.shape[-1] // groups
    entries = groups * capacity
    rows = groups * GROUP_ROWS
    seg = nb // side
    reductions = 2 * ITERS - 1
    slots = -(-owner_slot.shape[0] // 2048) * 2048
    owner = jnp.pad(owner_slot, (0, slots - owner_slot.shape[0])).reshape(-1, HALF)
    vmem = pl.BlockSpec(memory_space=pltpu.VMEM)
    out = jax.ShapeDtypeStruct((points // HALF, HALF), F32)
    dma = pltpu.SemaphoreType.DMA
    tall = 6 * GROUP_ROWS
    source_pot, target_pot = pl.pallas_call(
        functools.partial(kernel, groups, side, capacity, nb),
        out_shape=(out, out),
        in_specs=[vmem] * 7,
        out_specs=(vmem, vmem),
        scratch_shapes=[
            *[pltpu.VMEM((groups, GROUP_ROWS, HALF), jnp.int32)] * 3,
            pltpu.VMEM((2, capacity, groups, HALF), jnp.int32),
            pltpu.VMEM((2, 2, side, GROUP_ROWS, HALF), jnp.int32),
            pltpu.VMEM((2, 2, side, nb, HALF), BF16),
            pltpu.VMEM((2, 2, side * entries, nb), BF16),
            *[pltpu.VMEM((rows, nb), BF16)] * 2,
            pltpu.VMEM((4, 3, nb, BS), BF16),
            pltpu.VMEM((3, groups, GROUP_ROWS, BS), F32),
            *[pltpu.VMEM((groups, 4, GROUP_ROWS, BS), F32)] * 2,
            *[pltpu.VMEM((entries, GROUP_ROWS, BS), F32)] * 2,
            *[pltpu.VMEM((entries, tall, BS), BF16)] * 3,
            *[pltpu.VMEM((2, groups, GROUP_ROWS, HALF), F32)] * 7,
            *[pltpu.VMEM((capacity, groups, HALF), F32)] * 2,
            *[pltpu.VMEM((ITERS, 2, groups, GROUP_ROWS, HALF), F32)] * 2,
            pltpu.VMEM((reductions, 2, capacity, groups, HALF), F32),
            pltpu.VMEM((reductions, 2, side, capacity, groups, HALF), F32),
            pltpu.VMEM((side, nb, HALF), F32),
            pltpu.VMEM((2, nb, HALF), F32),
            *[pltpu.VMEM((reductions, 2, side, capacity, groups, HALF), F32)] * 2,
            pltpu.VMEM((2, nb, HALF), F32),
            pltpu.VMEM((2, side, seg, HALF), F32),
            pltpu.VMEM((2, 2, side, seg, HALF), F32),
            pltpu.VMEM((2, 2, nb, HALF), F32),
            dma((2,)),
            dma((2, 2, 2)),
            dma,
            dma((groups,)),
            dma((2,)),
            dma((2, groups)),
            dma((ITERS, 2, 2)),
            dma((reductions, 2, 2, 2)),
            dma((2, 2, 3, 2)),
        ],
        compiler_params=pltpu.CompilerParams(
            collective_id=0, has_side_effects=True, vmem_limit_bytes=40 * 1024 * 1024
        ),
        name="sinkhorn",
    )(
        pairs[0, 0], owner,
        source_points.reshape(3, nb, BS), target_points.reshape(3, nb, BS),
        source_logw.reshape(-1, HALF), target_logw.reshape(-1, HALF), warm_start.reshape(-1, HALF),
    )
    return source_pot.reshape(-1), target_pot.reshape(-1)


def solution(mesh):
    return jax.shard_map(
        per_device,
        mesh=mesh,
        in_specs=(
            P(None, "blk"),
            P(None, "blk"),
            P("blk"),
            P("blk"),
            P("blk"),
            P("blk", "pair", None, None),
            P(),
        ),
        out_specs=(P("blk"), P("blk")),
        check_vma=False,
    )
```

```python
import functools

import jax
import jax.numpy as jnp
from jax import lax
from jax.experimental import pallas as pl
from jax.experimental.pallas import tpu as pltpu
from jax.sharding import PartitionSpec as P

BS = 256
HALF = 128
ITERS = 2
BATCH = 4
GROUP_ROWS = 8
LOG2E = 1.4426950408889634
LN2 = 0.6931471805599453
EPSILON = 0.5
INV_EPS2 = LOG2E / EPSILON
LOW = -1e30
MESH = pl.DeviceIdType.MESH
F32 = jnp.float32
BF16 = jnp.bfloat16


def log2(value):
    return jnp.log(value) * LOG2E


def split3(value):
    high = value.astype(BF16).astype(F32)
    rest = value - high
    middle = rest.astype(BF16).astype(F32)
    return high, middle, rest - middle


def left_parts(value):
    one, two, three = split3(value)
    return jnp.concatenate((one, one, two, two, one, three), axis=0).astype(BF16)


def right_parts(value):
    one, two, three = split3(value)
    return jnp.concatenate((one, two, one, two, three, one), axis=0).astype(BF16)


def tile_lse(left, right):
    terms = lax.dot_general(left, right, (((0,), (0,)), ((), ())), preferred_element_type=F32)
    top = jnp.max(terms, axis=0, keepdims=True)
    return top + log2(jnp.sum(jnp.exp2(terms - top), axis=0, keepdims=True))


def lse_pair(first, second):
    top = jnp.maximum(first, second)
    return top + log2(jnp.exp2(first - top) + jnp.exp2(second - top))


def tile_all(lefts, rights):
    return [tile_lse(one, two) for one, two in zip(lefts, rights)]


def gather(hot, parts):
    total = None
    for part in parts:
        one = jnp.dot(hot, part.astype(BF16), preferred_element_type=F32)
        total = one if total is None else total + one
    return total


def lanes_of(h):
    return slice(h * HALF, (h + 1) * HALF)


def wait_bytes(ref, sem):
    pltpu.make_async_copy(ref, ref, sem).wait()


def far_first(k, size):
    return size // 2 + (1 - 2 * (k % 2)) * ((k + 1) // 2)


def kernel(
    groups, side, capacity, nb,
    pairs_v, owner, *operands_and_rest,
):
    inputs, rest = operands_and_rest[:5], operands_and_rest[5:]
    held, rest = rest[2:7], rest[:2] + rest[7:]
    run(groups, side, capacity, nb, pairs_v, owner, inputs, held, *rest)


def run(
    groups, side, capacity, nb, pairs_v, owner, inputs, held,
    out_src, out_tgt, src_blocks, tgt_blocks, input_sem,
    ids_send, ids_src, ids_tgt, own_ids, lists, place, pick, pick_src, pick_tgt, table,
    got_src, got_send, got_recv, src_pack, tgt_pack, left, right_src, right_tgt,
    mass_src, mass_tgt, bias, send_pot, recv_pot, terms, partial, values_c, merged, send_col, recv_col,
    spread, spread_got, placed, row_sum, asked, asked_got, dense, stage1, stage2, full,
    ids_sem, list_sem, pack_sent, pack_sem, pot_sent, pot_sem, col_sem, spread_sem, red_sem,
):
    b = lax.axis_index("blk")
    p = lax.axis_index("pair")
    z, y = p // side, p % side
    rows = groups * GROUP_ROWS
    seg = nb // side
    chips = groups // 2

    def blk_index(k):
        x = lax.rem(b // 2 + far_first(k // 2, chips), chips)
        return x * 2 + lax.rem(b + 1 + k, 2)

    def near(k):
        return blk_index(groups - 1 - k)

    def y_index(k):
        return z * side + lax.rem(y + far_first(k, side), side)

    def z_index(k):
        return lax.rem(z + far_first(k, side), side) * side + y

    copies = []
    for i, (outside, inside) in enumerate(zip(inputs, held)):
        copies.append(pltpu.make_async_copy(outside, inside, input_sem.at[i]))
        copies[i].start()
    tgt_pts, tgt_mass, warm, src_pts, src_mass = held

    barrier = pltpu.get_barrier_semaphore()

    def greet(axis, index, count):
        def one(k, carry):
            pl.semaphore_signal(barrier, inc=1, device_id={axis: index(k)}, device_id_type=MESH)
            return carry

        lax.fori_loop(0, count - 1, one, 0)

    greet("blk", blk_index, groups)
    greet("pair", y_index, side)
    greet("pair", z_index, side)

    def send(axis, peer, src, dst, sent, arrived):
        pltpu.make_async_remote_copy(
            src_ref=src, dst_ref=dst, send_sem=sent, recv_sem=arrived,
            device_id={axis: peer}, device_id_type=MESH,
        ).start()

    entries = groups * capacity
    row = lax.broadcasted_iota(jnp.int32, (rows, HALF), 0)
    lane = lax.broadcasted_iota(jnp.int32, (rows, HALF), 1)
    group, member = row // GROUP_ROWS, row % GROUP_ROWS
    listed = member < capacity
    own_lane = jnp.where(listed, group * capacity + member, -1)[:, :entries] == lane[:, :entries]

    def column(values):
        picked = jnp.where(own_lane, values.astype(F32), 0.0)
        total = jnp.sum(picked, axis=1, keepdims=True)
        return jnp.broadcast_to(total, (rows, HALF)).astype(jnp.int32)

    shape_ids = (groups, GROUP_ROWS, HALF)
    source_id = column(pairs_v[0:1, :])
    target_id = column(pairs_v[1:2, :])
    live = listed & (target_id >= 0)
    ids_src[...] = jnp.where(live, source_id - b * nb, -1).reshape(shape_ids)
    table_rows = owner.shape[0]
    high = jnp.where(target_id[:, :table_rows] // HALF == lane[:, :table_rows], 1.0, 0.0)
    slot = gather(high.astype(BF16), split3(owner[...].astype(F32)))
    slot = jnp.sum(jnp.where(target_id % HALF == lane, slot, 0.0), axis=1, keepdims=True)
    slot = jnp.broadcast_to(slot, (rows, HALF)).astype(jnp.int32)
    ids_send[...] = jnp.where(live, slot - group * nb, -1).reshape(shape_ids)

    def by_blocks(points, blocks):
        def eight(q, carry):
            for r in range(GROUP_ROWS):
                first = pl.multiple_of((q * GROUP_ROWS + r) * BS, BS)
                value = points[:, pl.ds(first, BS)]
                for i in range(3):
                    blocks[i, q, r : r + 1, :] = value[i : i + 1, :]
            return carry

        lax.fori_loop(0, nb // GROUP_ROWS, eight, 0)

    def vector_half(ref, h):
        return ref[pl.ds(h, nb, stride=2), :]

    copies[0].wait()
    by_blocks(tgt_pts, tgt_blocks)
    for i in range(3):
        for j, part in enumerate(split3(tgt_blocks[i].reshape(nb, BS))):
            table[i, j] = part.astype(BF16)
    copies[1].wait()
    copies[2].wait()
    for h in range(2):
        first = vector_half(tgt_mass, h) * LOG2E + vector_half(warm, h) * INV_EPS2
        for j, part in enumerate(split3(first)):
            table[3, j, :, lanes_of(h)] = part.astype(BF16)

    pl.semaphore_wait(barrier, groups - 1 + 2 * (side - 1))

    def send_ids(k, carry):
        g = blk_index(k)
        send("blk", g, ids_send.at[g], ids_tgt.at[b], ids_sem.at[0], ids_sem.at[1])
        return carry

    lax.fori_loop(0, groups - 1, send_ids, 0)
    ids_tgt[b] = ids_send[b]

    def pick_matrix(ids, pick):
        ids = ids[...].reshape(rows, HALF)
        wide = jnp.concatenate([ids] * (nb // HALF), axis=1) if nb > HALF else ids[:, :nb]
        match = wide == lax.broadcasted_iota(jnp.int32, (rows, nb), 1)
        pick[...] = jnp.where(match, 1.0, 0.0).astype(BF16)

    lane_row = lane % entries
    lane_place = (lane_row % groups) * GROUP_ROWS + lane_row // groups

    def make_list(ids):
        ids = ids[...].reshape(rows, HALF).astype(F32)
        inside = lane < 3 * entries
        lanes = jnp.sum(jnp.where((row == lane_place) & inside, ids, 0.0), axis=0, keepdims=True)
        before = listed & (member * groups + group < lane_row)
        again = jnp.max(jnp.where((ids == lanes) & before, 1.0, 0.0), axis=0, keepdims=True)
        once = jnp.where((again > 0.0) | jnp.logical_not(inside[0:1, :]), -1.0, lanes)
        line = lax.broadcasted_iota(jnp.int32, (GROUP_ROWS, HALF), 0)
        return jnp.where(line == 0, lanes, jnp.where(line == 1, once, -1.0)).astype(jnp.int32)

    def send_list(s):
        for axis, (index, mine) in enumerate(((y_index, y), (z_index, z))):
            spot = lists.at[s, axis, mine]

            def one(k, carry, index=index, spot=spot, axis=axis):
                sems = list_sem.at[s, axis]
                send("pair", index(k), spot, spot, sems.at[0], sems.at[1])
                return carry

            lax.fori_loop(0, side - 1, one, 0)

    def read_lists(s):
        block = lax.broadcasted_iota(jnp.int32, (nb, HALF), 0)
        lane_nb = lax.broadcasted_iota(jnp.int32, (nb, HALF), 1)
        ones = jnp.ones((HALF, HALF), BF16)
        row_e = lax.broadcasted_iota(jnp.int32, (entries, HALF), 0)
        lane_e = lax.broadcasted_iota(jnp.int32, (entries, HALF), 1)
        for axis in range(2):
            wait_bytes(lists.at[s, axis, pl.ds(0, side - 1)], list_sem.at[s, axis, 1])

            def one(i, carry, axis=axis):
                match = jnp.where(block == lists[s, axis, i, 1:2, :], 1.0, 0.0)
                count = jnp.dot(match.astype(BF16), ones, preferred_element_type=F32)
                none = jnp.where(count > 0.5, 0.0, 1.0)
                place[s, axis, i] = jnp.where(lane_nb == 3 * entries, none, match).astype(BF16)
                return carry

            lax.fori_loop(0, side, one, 0)
            columns = []
            for i in range(side):
                ids = jnp.where(row_e == lane_e, lists[s, axis, i, 0:1, :], 0).astype(F32)
                ids = jnp.sum(ids, axis=1, keepdims=True)
                columns.append(jnp.broadcast_to(ids, (entries, HALF)).astype(jnp.int32))
            ids = jnp.concatenate(columns, axis=0)
            wide = jnp.concatenate([ids] * (nb // HALF), axis=1) if nb > HALF else ids[:, :nb]
            match = wide == lax.broadcasted_iota(jnp.int32, (side * entries, nb), 1)
            pick[s, axis] = jnp.where(match, 1.0, 0.0).astype(BF16)

    def to_compact(ref, target):
        for c in range(capacity):
            for g in range(groups):
                target[c, g : g + 1, :] = ref[g, c : c + 1, :]

    def to_wide(values, target):
        for c in range(capacity):
            for g in range(groups):
                target[g, c : c + 1, :] = values[c, g : g + 1, :]

    row8 = lax.broadcasted_iota(jnp.int32, (GROUP_ROWS, BS), 0)
    row8_half = lax.broadcasted_iota(jnp.int32, (GROUP_ROWS, HALF), 0)

    def pack_rows(points, scale, flipped, bias_row):
        square = points[0] * points[0] + points[1] * points[1] + points[2] * points[2]
        norm = square * (-INV_EPS2)
        lines = [point * scale for point in points]
        lines += [1.0, norm] if flipped else [norm, 1.0]
        lines.append(bias_row)
        packed = jnp.zeros((GROUP_ROWS, BS), F32)
        for r, line in enumerate(lines):
            packed = jnp.where(row8 == r, line, packed)
        return packed

    def own_list(s, ids):
        tile = make_list(ids)
        lists[s, 0, y] = tile
        lists[s, 1, z] = tile
        send_list(s)
        to_compact(ids, own_ids.at[s])

    low_half = jnp.full(shape_ids, LOW, F32)
    for h in range(2):
        terms[h] = low_half
        partial[h] = low_half
        send_pot[h] = low_half
    shape3 = (groups, GROUP_ROWS, BS)
    own_list(0, ids_src)
    pick_matrix(ids_src, pick_src)
    copies[3].wait()
    copies[4].wait()
    by_blocks(src_pts, src_blocks)
    for i in range(3):
        points = src_blocks[i].reshape(nb, BS)
        got_src[i] = gather(pick_src[...], split3(points)).reshape(shape3)

    wait_bytes(ids_tgt.at[pl.ds(0, groups - 1)], ids_sem.at[1])
    pick_matrix(ids_tgt, pick_tgt)
    for i in range(4):
        found = gather(pick_tgt[...], [table[i, j] for j in range(3)]).reshape(shape3)
        for g in range(groups):
            got_send[g, i] = found[g]

    def send_pack(k, carry):
        g = blk_index(k)
        send("blk", g, got_send.at[g], got_recv.at[b], pack_sent, pack_sem.at[b])
        return carry

    lax.fori_loop(0, groups - 1, send_pack, 0)
    got_recv[b] = got_send[b]

    def source_group(g, carry):
        for c in range(capacity):
            k = g * capacity + c
            points = [got_src[i, g, c : c + 1, :] for i in range(3)]
            packed = pack_rows(points, 2.0 * INV_EPS2, True, 1.0)
            src_pack[k] = packed
            right_src[k] = right_parts(packed)
        return carry

    lax.fori_loop(0, groups, source_group, 0)
    own_list(1, ids_tgt)
    for h in range(2):
        found = gather(pick_src[...], split3(vector_half(src_mass, h) * LOG2E))
        mass_src[h] = found.reshape(shape_ids)
        found = gather(pick_tgt[...], split3(vector_half(tgt_mass, h) * LOG2E))
        mass_tgt[h] = found.reshape(shape_ids)

    def merge(s, values, target):
        to_compact(values, values_c)

        for c in range(capacity):
            for g in range(groups):
                same = own_ids[s].reshape(entries, HALF) == own_ids[s, c, g : g + 1, :]
                picked = jnp.where(same, values_c[...].reshape(entries, HALF), LOW)
                top = jnp.max(picked, axis=0, keepdims=True)
                total = jnp.sum(jnp.exp2(picked - top), axis=0, keepdims=True)
                target[c, g : g + 1, :] = top + log2(total)

    def put(matrix, values):
        one, two, three = split3(values.reshape(entries, HALF))
        none = jnp.full((HALF - 3 * entries, HALF), LOW, F32)
        parts = jnp.concatenate((one, two, three, none), axis=0).astype(BF16)
        return jnp.dot(matrix, parts, preferred_element_type=F32)

    places = (y, z)
    firsts = (y_index, z_index)
    seconds = (z_index, y_index)

    def coordinate(h, peer):
        return lax.rem(peer, side) if h == 0 else peer // side

    def spread_start(a, h):
        mine = places[h]
        sems = spread_sem.at[a, h, 0]

        def one(k, carry):
            send("pair", firsts[h](k), spread.at[a, h], spread_got.at[a, h, mine], sems.at[0], sems.at[1])
            return carry

        lax.fori_loop(0, side - 1, one, 0)
        spread_got[a, h, mine] = spread[a, h]

    def spread_second(a, h, s):
        wait_bytes(spread_got.at[a, h, pl.ds(0, side - 1)], spread_sem.at[a, h, 0, 1])
        for i in range(side):
            placed[i] = put(place[s, h, i], spread_got[a, h, i])
        step = min(nb, 64)
        for q in range(nb // step):
            arrived = placed[:, q * step : (q + 1) * step, :]
            top = jnp.max(arrived, axis=0)
            total = jnp.sum(jnp.exp2(arrived - top[None]), axis=0)
            row_sum[h, q * step : (q + 1) * step, :] = top + log2(total)
        found = gather(pick[s, 1 - h], split3(row_sum[h]))
        asked[a, h] = found.reshape(side, capacity, groups, HALF)
        other = places[1 - h]
        sems = spread_sem.at[a, h, 1]

        def one(k, carry):
            peer = seconds[h](k)
            spot = asked.at[a, h, coordinate(1 - h, peer)]
            send("pair", peer, spot, asked_got.at[a, h, other], sems.at[0], sems.at[1])
            return carry

        lax.fori_loop(0, side - 1, one, 0)
        asked_got[a, h, other] = asked[a, h, other]

    def spread_end(a, h):
        wait_bytes(asked_got.at[a, h, pl.ds(0, side - 1)], spread_sem.at[a, h, 1, 1])
        arrived = asked_got[a, h]
        top = jnp.maximum(jnp.max(arrived, axis=0), 0.0)
        total = jnp.exp2(-top) + jnp.sum(jnp.exp2(arrived - top[None]), axis=0)
        return top + log2(total)

    def own_chunk(h):
        return pl.ds(pl.multiple_of(places[h] * seg, seg), seg)

    def reduce_start(h):
        mine = places[h]

        def one(k, carry):
            peer = firsts[h](k)
            chunk = pl.ds(pl.multiple_of(coordinate(h, peer) * seg, seg), seg)
            sems = red_sem.at[1, h, 0]
            send("pair", peer, dense.at[h, chunk], stage1.at[h, mine], sems.at[0], sems.at[1])
            return carry

        lax.fori_loop(0, side - 1, one, 0)
        stage1[h, mine] = dense[h, own_chunk(h), :]

    def reduce_second(o, h):
        other = places[1 - h]
        if o == 0:
            stage2[o, h, other] = row_sum[h, own_chunk(h), :]
        else:
            wait_bytes(stage1.at[h, pl.ds(0, side - 1)], red_sem.at[o, h, 0, 1])
            arrived = stage1[h]
            top = jnp.max(arrived, axis=0)
            stage2[o, h, other] = top + log2(jnp.sum(jnp.exp2(arrived - top[None]), axis=0))
        sems = red_sem.at[o, h, 1]

        def one(k, carry):
            spot = stage2.at[o, h, other]
            send("pair", seconds[h](k), spot, spot, sems.at[0], sems.at[1])
            return carry

        lax.fori_loop(0, side - 1, one, 0)

    def reduce_third(o, h):
        wait_bytes(stage2.at[o, h, pl.ds(0, side - 1)], red_sem.at[o, h, 1, 1])
        arrived = stage2[o, h]
        top = jnp.maximum(jnp.max(arrived, axis=0), 0.0)
        total = jnp.exp2(-top) + jnp.sum(jnp.exp2(arrived - top[None]), axis=0)
        full[o, h, own_chunk(h), :] = top + log2(total)
        sems = red_sem.at[o, h, 2]

        def one(k, carry):
            spot = full.at[o, h, own_chunk(h)]
            send("pair", firsts[h](k), spot, spot, sems.at[0], sems.at[1])
            return carry

        lax.fori_loop(0, side - 1, one, 0)

    def reduce_end(o, h, out):
        wait_bytes(full.at[o, h, pl.ds(0, (side - 1) * seg)], red_sem.at[o, h, 2, 1])
        out[pl.ds(h, nb, stride=2), :] = full[o, h] * (-EPSILON * LN2)

    def entries_of(gs):
        return [(g, c, g * capacity + c) for g in gs for c in range(capacity)]

    def in_batches(step, size):
        def one(i, carry):
            step([near(size * i + j) for j in range(size)])
            return carry

        lax.fori_loop(0, groups // size, one, 0)

    def as_they_come(step, ref, sem, size):
        def batch(i, first):
            gs = [near(size * i + j) for j in range(size)]
            for g in gs[first:]:
                wait_bytes(ref.at[g], sem.at[g])
            step(gs)

        def one(i, carry):
            batch(i, 0)
            return carry

        batch(0, 1)
        lax.fori_loop(1, groups // size, one, 0)

    many = min(BATCH, groups)

    def store_rows(ref, where, totals):
        for (g, c, k), total in zip(where, totals):
            ref[g, c : c + 1, :] = total

    def first_rows(gs):
        where = entries_of(gs)
        packs = []
        for g, c, k in where:
            points = [got_recv[g, i, c : c + 1, :] for i in range(3)]
            packs.append(pack_rows(points, 1.0, False, got_recv[g, 3, c : c + 1, :]))
        lefts = [left_parts(packed) for packed in packs]
        totals = tile_all(lefts, [right_src[k, :, lanes_of(0)] for g, c, k in where])
        for (g, c, k), packed, here in zip(where, packs, lefts):
            tgt_pack[k] = packed
            left[k] = here
        store_rows(terms.at[0], where, totals)

    def second_rows(gs):
        where = entries_of(gs)
        lefts = [left[k] for g, c, k in where]
        store_rows(terms.at[1], where, tile_all(lefts, [right_src[k, :, lanes_of(1)] for g, c, k in where]))

    def row_lefts(h, where):
        return [
            left_parts(
                jnp.where(row8_half == 5, recv_pot[h, g, c : c + 1, :], tgt_pack[k, :, lanes_of(h)])
            )
            for g, c, k in where
        ]

    def store_halves(where, totals):
        for out in range(2):
            store_rows(partial.at[out], where, [total[:, lanes_of(out)] for total in totals])

    def early_rows(gs):
        where = entries_of(gs)
        store_halves(where, tile_all(row_lefts(0, where), [right_src[k] for g, c, k in where]))

    def late_rows(gs):
        where = entries_of(gs)
        lefts = row_lefts(1, where)
        totals = tile_all(lefts, [right_src[k, :, lanes_of(0)] for g, c, k in where])
        for (g, c, k), here in zip(where, lefts):
            left[k, :, lanes_of(1)] = here
        store_rows(terms.at[0], where, totals)

    def last_rows(gs):
        where = entries_of(gs)
        lefts = [left[k, :, lanes_of(1)] for g, c, k in where]
        store_rows(terms.at[1], where, tile_all(lefts, [right_src[k, :, lanes_of(1)] for g, c, k in where]))

    def column_lefts(h, where):
        return [
            left_parts(
                jnp.where(row8_half == 5, bias[h, g, c : c + 1, :], src_pack[k, :, lanes_of(h)])
            )
            for g, c, k in where
        ]

    def early_columns(gs):
        where = entries_of(gs)
        store_halves(where, tile_all(column_lefts(0, where), [right_tgt[k] for g, c, k in where]))

    def late_columns(it, out, gs):
        where = entries_of(gs)
        if out == 0:
            lefts = column_lefts(1, where)
        else:
            lefts = [left[k, :, lanes_of(1)] for g, c, k in where]
        totals = tile_all(lefts, [right_tgt[k, :, lanes_of(out)] for g, c, k in where])
        if out == 0:
            for (g, c, k), here in zip(where, lefts):
                left[k, :, lanes_of(1)] = here
        store_rows(terms.at[out], where, totals)
        for g in gs:
            send_col[it, out, g] = lse_pair(partial[out, g], terms[out, g])

    def target_group(gs):
        for g, c, k in entries_of(gs):
            right_tgt[k] = right_parts(jnp.where(row8 == 5, 1.0, tgt_pack[k]))

    for it in range(ITERS):
        a_src, a_tgt = 2 * it, 2 * it + 1
        last = it == ITERS - 1
        if it == 0:
            as_they_come(first_rows, got_recv, pack_sem, 2)
        else:
            for h in range(2):
                to_wide(spread_end(a_src - 1, h), send_pot.at[h])
                send_pot[h] = mass_tgt[h] - send_pot[h]

                def pot_send(k, carry, h=h):
                    g = blk_index(k)
                    send("blk", g, send_pot.at[h, g], recv_pot.at[h, b], pot_sent.at[h], pot_sem.at[h, b])
                    return carry

                lax.fori_loop(0, groups - 1, pot_send, 0)
                recv_pot[h, b] = send_pot[h, b]
            as_they_come(early_rows, recv_pot.at[0], pot_sem.at[0], many)
            as_they_come(late_rows, recv_pot.at[1], pot_sem.at[1], many)
            terms[0] = lse_pair(partial[0], terms[0])
        merge(0, terms.at[0], spread.at[a_src, 0])
        spread_start(a_src, 0)
        in_batches(second_rows if it == 0 else last_rows, many)
        if it > 0:
            terms[1] = lse_pair(partial[1], terms[1])
        merge(0, terms.at[1], spread.at[a_src, 1])
        spread_start(a_src, 1)
        if it == 0:
            read_lists(0)
        for h in range(2):
            spread_second(a_src, h, 0)
        if last:
            for h in range(2):
                reduce_second(0, h)
        if it == 0:
            in_batches(target_group, 2)
            read_lists(1)
        for h in range(2):
            to_wide(spread_end(a_src, h), bias.at[h])
            bias[h] = mass_src[h] - bias[h]
            if h == 0:
                in_batches(early_columns, many)
        for out in range(2):
            def send_columns(gs, count, out=out, it=it):
                late_columns(it, out, gs)
                sems = col_sem.at[it, out]
                for g in gs[:count]:
                    send(
                        "blk", g, send_col.at[it, out, g], recv_col.at[it, out, b],
                        sems.at[0], sems.at[1],
                    )

            def far_batch(i, carry, send_columns=send_columns):
                send_columns([blk_index(many * i + j) for j in range(many)], many)
                return carry

            lax.fori_loop(0, groups // many - 1, far_batch, 0)
            send_columns([near(many - 1 - j) for j in range(many)], many - 1)
            recv_col[it, out, b] = send_col[it, out, b]
        if last:
            for h in range(2):
                reduce_third(0, h)
        for out in range(2):
            wait_bytes(recv_col.at[it, out, pl.ds(0, groups - 1)], col_sem.at[it, out, 1])
            if last:
                merge(1, recv_col.at[it, out], merged)
                dense[out] = put(place[1, 0, y], merged[...])
                reduce_start(out)
            else:
                merge(1, recv_col.at[it, out], spread.at[a_tgt, out])
                spread_start(a_tgt, out)
        if not last:
            for h in range(2):
                spread_second(a_tgt, h, 1)

    for h in range(2):
        reduce_end(0, h, out_src)
    for step in (reduce_second, reduce_third):
        for h in range(2):
            step(1, h)
    def drain(sem, ref):
        wait_bytes(ref, sem)

    others = pl.ds(0, groups - 1)
    peers = pl.ds(0, side - 1)
    drain(ids_sem.at[0], ids_tgt.at[others])
    drain(pack_sent, got_recv.at[others])
    for h in range(2):
        if ITERS > 1:
            drain(pot_sent.at[h], recv_pot.at[h, others])
        for it in range(ITERS):
            drain(col_sem.at[it, h, 0], recv_col.at[it, h, others])
        for a in range(2 * ITERS - 1):
            for stage in range(2):
                drain(spread_sem.at[a, h, stage, 0], spread_got.at[a, h, peers])
        drain(red_sem.at[1, h, 0, 0], stage1.at[h, peers])
        for o in range(2):
            drain(red_sem.at[o, h, 1, 0], stage2.at[o, h, peers])
        drain(red_sem.at[0, h, 2, 0], stage1.at[h, peers])
        for s in range(2):
            drain(list_sem.at[s, h, 0], lists.at[s, h, peers])
    for h in range(2):
        reduce_end(1, h, out_tgt)
    for h in range(2):
        drain(red_sem.at[1, h, 2, 0], stage1.at[h, peers])


def per_device(
    source_points, target_points, source_logw, target_logw, warm_start, pairs, owner_slot
):
    groups = lax.axis_size("blk")
    side = round(lax.axis_size("pair") ** 0.5)
    points = source_logw.shape[0]
    nb = points // BS
    capacity = pairs.shape[-1] // groups
    entries = groups * capacity
    rows = groups * GROUP_ROWS
    seg = nb // side
    reductions = 2 * ITERS - 1
    slots = -(-owner_slot.shape[0] // 2048) * 2048
    owner = jnp.pad(owner_slot, (0, slots - owner_slot.shape[0])).reshape(-1, HALF)
    vmem = pl.BlockSpec(memory_space=pltpu.VMEM)
    out = jax.ShapeDtypeStruct((points // HALF, HALF), F32)
    dma = pltpu.SemaphoreType.DMA
    tall = 6 * GROUP_ROWS
    source_pot, target_pot = pl.pallas_call(
        functools.partial(kernel, groups, side, capacity, nb),
        out_shape=(out, out),
        in_specs=[vmem] * 2 + [pl.BlockSpec(memory_space=pl.ANY)] * 5,
        out_specs=(vmem, vmem),
        scratch_shapes=[
            pltpu.VMEM((3, points), F32),
            *[pltpu.VMEM((points // HALF, HALF), F32)] * 2,
            pltpu.VMEM((3, points), F32),
            pltpu.VMEM((points // HALF, HALF), F32),
            *[pltpu.VMEM((3, nb // GROUP_ROWS, GROUP_ROWS, BS), F32)] * 2,
            dma((5,)),
            *[pltpu.VMEM((groups, GROUP_ROWS, HALF), jnp.int32)] * 3,
            pltpu.VMEM((2, capacity, groups, HALF), jnp.int32),
            pltpu.VMEM((2, 2, side, GROUP_ROWS, HALF), jnp.int32),
            pltpu.VMEM((2, 2, side, nb, HALF), BF16),
            pltpu.VMEM((2, 2, side * entries, nb), BF16),
            *[pltpu.VMEM((rows, nb), BF16)] * 2,
            pltpu.VMEM((4, 3, nb, BS), BF16),
            pltpu.VMEM((3, groups, GROUP_ROWS, BS), F32),
            *[pltpu.VMEM((groups, 4, GROUP_ROWS, BS), F32)] * 2,
            *[pltpu.VMEM((entries, GROUP_ROWS, BS), F32)] * 2,
            *[pltpu.VMEM((entries, tall, BS), BF16)] * 3,
            *[pltpu.VMEM((2, groups, GROUP_ROWS, HALF), F32)] * 7,
            *[pltpu.VMEM((capacity, groups, HALF), F32)] * 2,
            *[pltpu.VMEM((ITERS, 2, groups, GROUP_ROWS, HALF), F32)] * 2,
            pltpu.VMEM((reductions, 2, capacity, groups, HALF), F32),
            pltpu.VMEM((reductions, 2, side, capacity, groups, HALF), F32),
            pltpu.VMEM((side, nb, HALF), F32),
            pltpu.VMEM((2, nb, HALF), F32),
            *[pltpu.VMEM((reductions, 2, side, capacity, groups, HALF), F32)] * 2,
            pltpu.VMEM((2, nb, HALF), F32),
            pltpu.VMEM((2, side, seg, HALF), F32),
            pltpu.VMEM((2, 2, side, seg, HALF), F32),
            pltpu.VMEM((2, 2, nb, HALF), F32),
            dma((2,)),
            dma((2, 2, 2)),
            dma,
            dma((groups,)),
            dma((2,)),
            dma((2, groups)),
            dma((ITERS, 2, 2)),
            dma((reductions, 2, 2, 2)),
            dma((2, 2, 3, 2)),
        ],
        compiler_params=pltpu.CompilerParams(
            collective_id=0, has_side_effects=True, vmem_limit_bytes=56832 * 1024
        ),
        name="sinkhorn",
    )(
        pairs[0, 0], owner,
        target_points, target_logw.reshape(-1, HALF), warm_start.reshape(-1, HALF),
        source_points, source_logw.reshape(-1, HALF),
    )
    return source_pot.reshape(-1), target_pot.reshape(-1)


def solution(mesh):
    return jax.shard_map(
        per_device,
        mesh=mesh,
        in_specs=(
            P(None, "blk"),
            P(None, "blk"),
            P("blk"),
            P("blk"),
            P("blk"),
            P("blk", "pair", None, None),
            P(),
        ),
        out_specs=(P("blk"), P("blk")),
        check_vma=False,
    )
```

```python
import functools

import jax
import jax.numpy as jnp
from jax import lax
from jax.experimental import pallas as pl
from jax.experimental.pallas import tpu as pltpu
from jax.sharding import PartitionSpec as P

BS = 256
HALF = 128
ITERS = 2
BATCH = 4
GROUP_ROWS = 8
LOG2E = 1.4426950408889634
LN2 = 0.6931471805599453
EPSILON = 0.5
INV_EPS2 = LOG2E / EPSILON
LOW = -1e30
MESH = pl.DeviceIdType.MESH
F32 = jnp.float32
BF16 = jnp.bfloat16


def log2(value):
    return jnp.log(value) * LOG2E


def split3(value):
    high = value.astype(BF16).astype(F32)
    rest = value - high
    middle = rest.astype(BF16).astype(F32)
    return high, middle, rest - middle


def left_parts(value):
    one, two, three = split3(value)
    return jnp.concatenate((one, one, two, two, one, three), axis=0).astype(BF16)


def right_parts(value):
    one, two, three = split3(value)
    return jnp.concatenate((one, two, one, two, three, one), axis=0).astype(BF16)


def tile_lse(left, right):
    terms = lax.dot_general(left, right, (((0,), (0,)), ((), ())), preferred_element_type=F32)
    top = jnp.max(terms, axis=0, keepdims=True)
    return top + log2(jnp.sum(jnp.exp2(terms - top), axis=0, keepdims=True))


def lse_pair(first, second):
    top = jnp.maximum(first, second)
    return top + log2(jnp.exp2(first - top) + jnp.exp2(second - top))


def tile_all(lefts, rights):
    return [tile_lse(one, two) for one, two in zip(lefts, rights)]


def gather(hot, parts):
    total = None
    for part in parts:
        one = jnp.dot(hot, part.astype(BF16), preferred_element_type=F32)
        total = one if total is None else total + one
    return total


def lanes_of(h):
    return slice(h * HALF, (h + 1) * HALF)


def wait_bytes(ref, sem):
    pltpu.make_async_copy(ref, ref, sem).wait()


def far_first(k, size):
    return size // 2 + (1 - 2 * (k % 2)) * ((k + 1) // 2)


def kernel(
    groups, side, capacity, nb,
    pairs_v, owner, *operands_and_rest,
):
    inputs, rest = operands_and_rest[:5], operands_and_rest[5:]
    held, rest = rest[2:7], rest[:2] + rest[7:]
    run(groups, side, capacity, nb, pairs_v, owner, inputs, held, *rest)


def run(
    groups, side, capacity, nb, pairs_v, owner, inputs, held,
    out_src, out_tgt, src_blocks, tgt_blocks, input_sem,
    ids_send, ids_src, ids_tgt, own_ids, lists, place, pick, pick_src, pick_tgt, table,
    got_src, got_send, got_recv, src_pack, tgt_pack, left, right_src, right_tgt,
    mass_src, mass_tgt, bias, send_pot, recv_pot, terms, partial, values_c, merged, send_col, recv_col,
    spread, spread_got, placed, row_sum, asked, asked_got, dense, stage1, stage2, full,
    ids_sem, list_sem, pack_sent, pack_sem, pot_sent, pot_sem, col_sem, spread_sem, red_sem,
):
    b = lax.axis_index("blk")
    p = lax.axis_index("pair")
    z, y = p // side, p % side
    rows = groups * GROUP_ROWS
    seg = nb // side
    chips = groups // 2

    def blk_index(k):
        x = lax.rem(b // 2 + far_first(k // 2, chips), chips)
        return x * 2 + lax.rem(b + 1 + k, 2)

    def near(k):
        return blk_index(groups - 1 - k)

    def y_index(k):
        return z * side + lax.rem(y + far_first(k, side), side)

    def z_index(k):
        return lax.rem(z + far_first(k, side), side) * side + y

    copies = []
    for i, (outside, inside) in enumerate(zip(inputs, held)):
        copies.append(pltpu.make_async_copy(outside, inside, input_sem.at[i]))
        copies[i].start()
    tgt_pts, tgt_mass, warm, src_pts, src_mass = held

    barrier = pltpu.get_barrier_semaphore()

    def greet(axis, index, count):
        def one(k, carry):
            pl.semaphore_signal(barrier, inc=1, device_id={axis: index(k)}, device_id_type=MESH)
            return carry

        lax.fori_loop(0, count - 1, one, 0)

    greet("blk", blk_index, groups)
    greet("pair", y_index, side)
    greet("pair", z_index, side)

    def send(axis, peer, src, dst, sent, arrived):
        pltpu.make_async_remote_copy(
            src_ref=src, dst_ref=dst, send_sem=sent, recv_sem=arrived,
            device_id={axis: peer}, device_id_type=MESH,
        ).start()

    entries = groups * capacity
    row = lax.broadcasted_iota(jnp.int32, (rows, HALF), 0)
    lane = lax.broadcasted_iota(jnp.int32, (rows, HALF), 1)
    group, member = row // GROUP_ROWS, row % GROUP_ROWS
    listed = member < capacity
    own_lane = jnp.where(listed, group * capacity + member, -1)[:, :entries] == lane[:, :entries]

    def column(values):
        picked = jnp.where(own_lane, values.astype(F32), 0.0)
        total = jnp.sum(picked, axis=1, keepdims=True)
        return jnp.broadcast_to(total, (rows, HALF)).astype(jnp.int32)

    shape_ids = (groups, GROUP_ROWS, HALF)
    source_id = column(pairs_v[0:1, :])
    target_id = column(pairs_v[1:2, :])
    live = listed & (target_id >= 0)
    ids_src[...] = jnp.where(live, source_id - b * nb, -1).reshape(shape_ids)
    table_rows = owner.shape[0]
    high = jnp.where(target_id[:, :table_rows] // HALF == lane[:, :table_rows], 1.0, 0.0)
    slot = gather(high.astype(BF16), split3(owner[...].astype(F32)))
    slot = jnp.sum(jnp.where(target_id % HALF == lane, slot, 0.0), axis=1, keepdims=True)
    slot = jnp.broadcast_to(slot, (rows, HALF)).astype(jnp.int32)
    ids_send[...] = jnp.where(live, slot - group * nb, -1).reshape(shape_ids)

    def by_blocks(points, blocks):
        def eight(q, carry):
            for r in range(GROUP_ROWS):
                first = pl.multiple_of((q * GROUP_ROWS + r) * BS, BS)
                value = points[:, pl.ds(first, BS)]
                for i in range(3):
                    blocks[i, q, r : r + 1, :] = value[i : i + 1, :]
            return carry

        lax.fori_loop(0, nb // GROUP_ROWS, eight, 0)

    def vector_half(ref, h):
        return ref[pl.ds(h, nb, stride=2), :]

    copies[0].wait()
    by_blocks(tgt_pts, tgt_blocks)
    for i in range(3):
        for j, part in enumerate(split3(tgt_blocks[i].reshape(nb, BS))):
            table[i, j] = part.astype(BF16)
    copies[1].wait()
    copies[2].wait()
    for h in range(2):
        first = vector_half(tgt_mass, h) * LOG2E + vector_half(warm, h) * INV_EPS2
        for j, part in enumerate(split3(first)):
            table[3, j, :, lanes_of(h)] = part.astype(BF16)

    pl.semaphore_wait(barrier, groups - 1 + 2 * (side - 1))

    def send_ids(k, carry):
        g = blk_index(k)
        send("blk", g, ids_send.at[g], ids_tgt.at[b], ids_sem.at[0], ids_sem.at[1])
        return carry

    lax.fori_loop(0, groups - 1, send_ids, 0)
    ids_tgt[b] = ids_send[b]

    def pick_matrix(ids, pick):
        ids = ids[...].reshape(rows, HALF)
        wide = jnp.concatenate([ids] * (nb // HALF), axis=1) if nb > HALF else ids[:, :nb]
        match = wide == lax.broadcasted_iota(jnp.int32, (rows, nb), 1)
        pick[...] = jnp.where(match, 1.0, 0.0).astype(BF16)

    lane_row = lane % entries
    lane_place = (lane_row % groups) * GROUP_ROWS + lane_row // groups

    def make_list(ids):
        ids = ids[...].reshape(rows, HALF).astype(F32)
        inside = lane < 3 * entries
        lanes = jnp.sum(jnp.where((row == lane_place) & inside, ids, 0.0), axis=0, keepdims=True)
        before = listed & (member * groups + group < lane_row)
        again = jnp.max(jnp.where((ids == lanes) & before, 1.0, 0.0), axis=0, keepdims=True)
        once = jnp.where((again > 0.0) | jnp.logical_not(inside[0:1, :]), -1.0, lanes)
        line = lax.broadcasted_iota(jnp.int32, (GROUP_ROWS, HALF), 0)
        return jnp.where(line == 0, lanes, jnp.where(line == 1, once, -1.0)).astype(jnp.int32)

    def send_list(s):
        for axis, (index, mine) in enumerate(((y_index, y), (z_index, z))):
            spot = lists.at[s, axis, mine]

            def one(k, carry, index=index, spot=spot, axis=axis):
                sems = list_sem.at[s, axis]
                send("pair", index(k), spot, spot, sems.at[0], sems.at[1])
                return carry

            lax.fori_loop(0, side - 1, one, 0)

    def read_lists(s):
        block = lax.broadcasted_iota(jnp.int32, (nb, HALF), 0)
        lane_nb = lax.broadcasted_iota(jnp.int32, (nb, HALF), 1)
        ones = jnp.ones((HALF, HALF), BF16)
        row_e = lax.broadcasted_iota(jnp.int32, (entries, HALF), 0)
        lane_e = lax.broadcasted_iota(jnp.int32, (entries, HALF), 1)
        for axis in range(2):
            wait_bytes(lists.at[s, axis, pl.ds(0, side - 1)], list_sem.at[s, axis, 1])

            def one(i, carry, axis=axis):
                match = jnp.where(block == lists[s, axis, i, 1:2, :], 1.0, 0.0)
                count = jnp.dot(match.astype(BF16), ones, preferred_element_type=F32)
                none = jnp.where(count > 0.5, 0.0, 1.0)
                place[s, axis, i] = jnp.where(lane_nb == 3 * entries, none, match).astype(BF16)
                return carry

            lax.fori_loop(0, side, one, 0)
            columns = []
            for i in range(side):
                ids = jnp.where(row_e == lane_e, lists[s, axis, i, 0:1, :], 0).astype(F32)
                ids = jnp.sum(ids, axis=1, keepdims=True)
                columns.append(jnp.broadcast_to(ids, (entries, HALF)).astype(jnp.int32))
            ids = jnp.concatenate(columns, axis=0)
            wide = jnp.concatenate([ids] * (nb // HALF), axis=1) if nb > HALF else ids[:, :nb]
            match = wide == lax.broadcasted_iota(jnp.int32, (side * entries, nb), 1)
            pick[s, axis] = jnp.where(match, 1.0, 0.0).astype(BF16)

    def to_compact(ref, target):
        for c in range(capacity):
            for g in range(groups):
                target[c, g : g + 1, :] = ref[g, c : c + 1, :]

    def to_wide(values, target):
        for c in range(capacity):
            for g in range(groups):
                target[g, c : c + 1, :] = values[c, g : g + 1, :]

    row8 = lax.broadcasted_iota(jnp.int32, (GROUP_ROWS, BS), 0)
    row8_half = lax.broadcasted_iota(jnp.int32, (GROUP_ROWS, HALF), 0)

    def pack_rows(points, scale, flipped, bias_row):
        square = points[0] * points[0] + points[1] * points[1] + points[2] * points[2]
        norm = square * (-INV_EPS2)
        lines = [point * scale for point in points]
        lines += [1.0, norm] if flipped else [norm, 1.0]
        lines.append(bias_row)
        packed = jnp.zeros((GROUP_ROWS, BS), F32)
        for r, line in enumerate(lines):
            packed = jnp.where(row8 == r, line, packed)
        return packed

    def own_list(s, ids):
        tile = make_list(ids)
        lists[s, 0, y] = tile
        lists[s, 1, z] = tile
        send_list(s)
        to_compact(ids, own_ids.at[s])

    low_half = jnp.full(shape_ids, LOW, F32)
    for h in range(2):
        terms[h] = low_half
        partial[h] = low_half
        send_pot[h] = low_half
    shape3 = (groups, GROUP_ROWS, BS)
    own_list(0, ids_src)
    pick_matrix(ids_src, pick_src)
    copies[3].wait()
    copies[4].wait()
    by_blocks(src_pts, src_blocks)
    for i in range(3):
        points = src_blocks[i].reshape(nb, BS)
        got_src[i] = gather(pick_src[...], split3(points)).reshape(shape3)

    wait_bytes(ids_tgt.at[pl.ds(0, groups - 1)], ids_sem.at[1])
    pick_matrix(ids_tgt, pick_tgt)
    for i in range(4):
        found = gather(pick_tgt[...], [table[i, j] for j in range(3)]).reshape(shape3)
        for g in range(groups):
            got_send[g, i] = found[g]

    def send_pack(k, carry):
        g = blk_index(k)
        send("blk", g, got_send.at[g], got_recv.at[b], pack_sent, pack_sem.at[b])
        return carry

    lax.fori_loop(0, groups - 1, send_pack, 0)
    got_recv[b] = got_send[b]

    def source_group(g, carry):
        for c in range(capacity):
            k = g * capacity + c
            points = [got_src[i, g, c : c + 1, :] for i in range(3)]
            packed = pack_rows(points, 2.0 * INV_EPS2, True, 1.0)
            src_pack[k] = packed
            right_src[k] = right_parts(packed)
        return carry

    lax.fori_loop(0, groups, source_group, 0)
    own_list(1, ids_tgt)
    for h in range(2):
        found = gather(pick_src[...], split3(vector_half(src_mass, h) * LOG2E))
        mass_src[h] = found.reshape(shape_ids)
        found = gather(pick_tgt[...], split3(vector_half(tgt_mass, h) * LOG2E))
        mass_tgt[h] = found.reshape(shape_ids)

    def merge(s, values, target):
        to_compact(values, values_c)

        for c in range(capacity):
            for g in range(groups):
                same = own_ids[s].reshape(entries, HALF) == own_ids[s, c, g : g + 1, :]
                picked = jnp.where(same, values_c[...].reshape(entries, HALF), LOW)
                top = jnp.max(picked, axis=0, keepdims=True)
                total = jnp.sum(jnp.exp2(picked - top), axis=0, keepdims=True)
                target[c, g : g + 1, :] = top + log2(total)

    def put(matrix, values):
        one, two, three = split3(values.reshape(entries, HALF))
        none = jnp.full((HALF - 3 * entries, HALF), LOW, F32)
        parts = jnp.concatenate((one, two, three, none), axis=0).astype(BF16)
        return jnp.dot(matrix, parts, preferred_element_type=F32)

    places = (y, z)
    firsts = (y_index, z_index)
    seconds = (z_index, y_index)

    def coordinate(h, peer):
        return lax.rem(peer, side) if h == 0 else peer // side

    def spread_start(a, h):
        mine = places[h]
        sems = spread_sem.at[a, h, 0]

        def one(k, carry):
            send("pair", firsts[h](k), spread.at[a, h], spread_got.at[a, h, mine], sems.at[0], sems.at[1])
            return carry

        lax.fori_loop(0, side - 1, one, 0)
        spread_got[a, h, mine] = spread[a, h]

    def spread_second(a, h, s):
        wait_bytes(spread_got.at[a, h, pl.ds(0, side - 1)], spread_sem.at[a, h, 0, 1])
        for i in range(side):
            placed[i] = put(place[s, h, i], spread_got[a, h, i])
        step = min(nb, 64)
        for q in range(nb // step):
            arrived = placed[:, q * step : (q + 1) * step, :]
            top = jnp.max(arrived, axis=0)
            total = jnp.sum(jnp.exp2(arrived - top[None]), axis=0)
            row_sum[h, q * step : (q + 1) * step, :] = top + log2(total)
        found = gather(pick[s, 1 - h], split3(row_sum[h]))
        asked[a, h] = found.reshape(side, capacity, groups, HALF)
        other = places[1 - h]
        sems = spread_sem.at[a, h, 1]

        def one(k, carry):
            peer = seconds[h](k)
            spot = asked.at[a, h, coordinate(1 - h, peer)]
            send("pair", peer, spot, asked_got.at[a, h, other], sems.at[0], sems.at[1])
            return carry

        lax.fori_loop(0, side - 1, one, 0)
        asked_got[a, h, other] = asked[a, h, other]

    def spread_end(a, h):
        wait_bytes(asked_got.at[a, h, pl.ds(0, side - 1)], spread_sem.at[a, h, 1, 1])
        arrived = asked_got[a, h]
        top = jnp.maximum(jnp.max(arrived, axis=0), 0.0)
        total = jnp.exp2(-top) + jnp.sum(jnp.exp2(arrived - top[None]), axis=0)
        return top + log2(total)

    def own_chunk(h):
        return pl.ds(pl.multiple_of(places[h] * seg, seg), seg)

    def reduce_start(h):
        mine = places[h]

        def one(k, carry):
            peer = firsts[h](k)
            chunk = pl.ds(pl.multiple_of(coordinate(h, peer) * seg, seg), seg)
            sems = red_sem.at[1, h, 0]
            send("pair", peer, dense.at[h, chunk], stage1.at[h, mine], sems.at[0], sems.at[1])
            return carry

        lax.fori_loop(0, side - 1, one, 0)
        stage1[h, mine] = dense[h, own_chunk(h), :]

    def reduce_second(o, h):
        other = places[1 - h]
        if o == 0:
            stage2[o, h, other] = row_sum[h, own_chunk(h), :]
        else:
            wait_bytes(stage1.at[h, pl.ds(0, side - 1)], red_sem.at[o, h, 0, 1])
            arrived = stage1[h]
            top = jnp.max(arrived, axis=0)
            stage2[o, h, other] = top + log2(jnp.sum(jnp.exp2(arrived - top[None]), axis=0))
        sems = red_sem.at[o, h, 1]

        def one(k, carry):
            spot = stage2.at[o, h, other]
            send("pair", seconds[h](k), spot, spot, sems.at[0], sems.at[1])
            return carry

        lax.fori_loop(0, side - 1, one, 0)

    def reduce_third(o, h):
        wait_bytes(stage2.at[o, h, pl.ds(0, side - 1)], red_sem.at[o, h, 1, 1])
        arrived = stage2[o, h]
        top = jnp.maximum(jnp.max(arrived, axis=0), 0.0)
        total = jnp.exp2(-top) + jnp.sum(jnp.exp2(arrived - top[None]), axis=0)
        full[o, h, own_chunk(h), :] = top + log2(total)
        sems = red_sem.at[o, h, 2]

        def one(k, carry):
            spot = full.at[o, h, own_chunk(h)]
            send("pair", firsts[h](k), spot, spot, sems.at[0], sems.at[1])
            return carry

        lax.fori_loop(0, side - 1, one, 0)

    def reduce_end(o, h, out):
        wait_bytes(full.at[o, h, pl.ds(0, (side - 1) * seg)], red_sem.at[o, h, 2, 1])
        out[pl.ds(h, nb, stride=2), :] = full[o, h] * (-EPSILON * LN2)

    def entries_of(gs):
        return [(g, c, g * capacity + c) for g in gs for c in range(capacity)]

    def in_batches(step, size):
        def one(i, carry):
            step([near(size * i + j) for j in range(size)])
            return carry

        lax.fori_loop(0, groups // size, one, 0)

    def as_they_come(step, ref, sem, size):
        def batch(i, first):
            gs = [near(size * i + j) for j in range(size)]
            for g in gs[first:]:
                wait_bytes(ref.at[g], sem.at[g])
            step(gs)

        def one(i, carry):
            batch(i, 0)
            return carry

        batch(0, 1)
        lax.fori_loop(1, groups // size, one, 0)

    many = min(BATCH, groups)

    def store_rows(ref, where, totals):
        for (g, c, k), total in zip(where, totals):
            ref[g, c : c + 1, :] = total

    def first_rows(gs):
        where = entries_of(gs)
        packs = []
        for g, c, k in where:
            points = [got_recv[g, i, c : c + 1, :] for i in range(3)]
            packs.append(pack_rows(points, 1.0, False, got_recv[g, 3, c : c + 1, :]))
        lefts = [left_parts(packed) for packed in packs]
        totals = tile_all(lefts, [right_src[k, :, lanes_of(0)] for g, c, k in where])
        for (g, c, k), packed, here in zip(where, packs, lefts):
            tgt_pack[k] = packed
            left[k] = here
        store_rows(terms.at[0], where, totals)

    def second_rows(gs):
        where = entries_of(gs)
        lefts = [left[k] for g, c, k in where]
        store_rows(terms.at[1], where, tile_all(lefts, [right_src[k, :, lanes_of(1)] for g, c, k in where]))

    def row_lefts(h, where):
        return [
            left_parts(
                jnp.where(row8_half == 5, recv_pot[h, g, c : c + 1, :], tgt_pack[k, :, lanes_of(h)])
            )
            for g, c, k in where
        ]

    def store_halves(where, totals):
        for out in range(2):
            store_rows(partial.at[out], where, [total[:, lanes_of(out)] for total in totals])

    def early_rows(gs):
        where = entries_of(gs)
        store_halves(where, tile_all(row_lefts(0, where), [right_src[k] for g, c, k in where]))

    def late_rows(gs):
        where = entries_of(gs)
        lefts = row_lefts(1, where)
        totals = tile_all(lefts, [right_src[k, :, lanes_of(0)] for g, c, k in where])
        for (g, c, k), here in zip(where, lefts):
            left[k, :, lanes_of(1)] = here
        store_rows(terms.at[0], where, totals)

    def last_rows(gs):
        where = entries_of(gs)
        lefts = [left[k, :, lanes_of(1)] for g, c, k in where]
        store_rows(terms.at[1], where, tile_all(lefts, [right_src[k, :, lanes_of(1)] for g, c, k in where]))

    def column_lefts(h, where):
        return [
            left_parts(
                jnp.where(row8_half == 5, bias[h, g, c : c + 1, :], src_pack[k, :, lanes_of(h)])
            )
            for g, c, k in where
        ]

    def early_columns(gs):
        where = entries_of(gs)
        store_halves(where, tile_all(column_lefts(0, where), [right_tgt[k] for g, c, k in where]))

    def late_columns(it, out, gs):
        where = entries_of(gs)
        if out == 0:
            lefts = column_lefts(1, where)
        else:
            lefts = [left[k, :, lanes_of(1)] for g, c, k in where]
        totals = tile_all(lefts, [right_tgt[k, :, lanes_of(out)] for g, c, k in where])
        if out == 0:
            for (g, c, k), here in zip(where, lefts):
                left[k, :, lanes_of(1)] = here
        store_rows(terms.at[out], where, totals)
        for g in gs:
            send_col[it, out, g] = lse_pair(partial[out, g], terms[out, g])

    def all_columns(it, gs):
        where = entries_of(gs)
        totals = tile_all(column_lefts(1, where), [right_tgt[k] for g, c, k in where])
        for out in range(2):
            store_rows(terms.at[out], where, [total[:, lanes_of(out)] for total in totals])
            for g in gs:
                send_col[it, out, g] = lse_pair(partial[out, g], terms[out, g])

    def target_group(gs):
        for g, c, k in entries_of(gs):
            right_tgt[k] = right_parts(jnp.where(row8 == 5, 1.0, tgt_pack[k]))

    for it in range(ITERS):
        a_src, a_tgt = 2 * it, 2 * it + 1
        last = it == ITERS - 1
        if it == 0:
            as_they_come(first_rows, got_recv, pack_sem, 2)
        else:
            for h in range(2):
                to_wide(spread_end(a_src - 1, h), send_pot.at[h])
                send_pot[h] = mass_tgt[h] - send_pot[h]

                def pot_send(k, carry, h=h):
                    g = blk_index(k)
                    send("blk", g, send_pot.at[h, g], recv_pot.at[h, b], pot_sent.at[h], pot_sem.at[h, b])
                    return carry

                lax.fori_loop(0, groups - 1, pot_send, 0)
                recv_pot[h, b] = send_pot[h, b]
            as_they_come(early_rows, recv_pot.at[0], pot_sem.at[0], many)
            as_they_come(late_rows, recv_pot.at[1], pot_sem.at[1], many)
            terms[0] = lse_pair(partial[0], terms[0])
        merge(0, terms.at[0], spread.at[a_src, 0])
        spread_start(a_src, 0)
        in_batches(second_rows if it == 0 else last_rows, many)
        if it > 0:
            terms[1] = lse_pair(partial[1], terms[1])
        merge(0, terms.at[1], spread.at[a_src, 1])
        spread_start(a_src, 1)
        if it == 0:
            read_lists(0)
        for h in range(2):
            spread_second(a_src, h, 0)
        if last:
            for h in range(2):
                reduce_second(0, h)
        if it == 0:
            in_batches(target_group, 2)
            read_lists(1)
        for h in range(2):
            to_wide(spread_end(a_src, h), bias.at[h])
            bias[h] = mass_src[h] - bias[h]
            if h == 0:
                in_batches(early_columns, many)
        for outs in ((0, 1),) if last else ((0,), (1,)):
            def send_columns(gs, count, outs=outs, it=it):
                if len(outs) == 2:
                    all_columns(it, gs)
                else:
                    late_columns(it, outs[0], gs)
                for out in outs:
                    sems = col_sem.at[it, out]
                    for g in gs[:count]:
                        send(
                            "blk", g, send_col.at[it, out, g], recv_col.at[it, out, b],
                            sems.at[0], sems.at[1],
                        )

            def far_batch(i, carry, send_columns=send_columns):
                send_columns([blk_index(many * i + j) for j in range(many)], many)
                return carry

            lax.fori_loop(0, groups // many - 1, far_batch, 0)
            send_columns([near(many - 1 - j) for j in range(many)], many - 1)
            for out in outs:
                recv_col[it, out, b] = send_col[it, out, b]
        if last:
            for h in range(2):
                reduce_third(0, h)
        for out in range(2):
            wait_bytes(recv_col.at[it, out, pl.ds(0, groups - 1)], col_sem.at[it, out, 1])
            if last:
                merge(1, recv_col.at[it, out], merged)
                dense[out] = put(place[1, 0, y], merged[...])
                reduce_start(out)
            else:
                merge(1, recv_col.at[it, out], spread.at[a_tgt, out])
                spread_start(a_tgt, out)
        if not last:
            for h in range(2):
                spread_second(a_tgt, h, 1)

    for h in range(2):
        reduce_end(0, h, out_src)
    for step in (reduce_second, reduce_third):
        for h in range(2):
            step(1, h)
    def drain(sem, ref):
        wait_bytes(ref, sem)

    others = pl.ds(0, groups - 1)
    peers = pl.ds(0, side - 1)
    drain(ids_sem.at[0], ids_tgt.at[others])
    drain(pack_sent, got_recv.at[others])
    for h in range(2):
        if ITERS > 1:
            drain(pot_sent.at[h], recv_pot.at[h, others])
        for it in range(ITERS):
            drain(col_sem.at[it, h, 0], recv_col.at[it, h, others])
        for a in range(2 * ITERS - 1):
            for stage in range(2):
                drain(spread_sem.at[a, h, stage, 0], spread_got.at[a, h, peers])
        drain(red_sem.at[1, h, 0, 0], stage1.at[h, peers])
        for o in range(2):
            drain(red_sem.at[o, h, 1, 0], stage2.at[o, h, peers])
        drain(red_sem.at[0, h, 2, 0], stage1.at[h, peers])
        for s in range(2):
            drain(list_sem.at[s, h, 0], lists.at[s, h, peers])
    for h in range(2):
        reduce_end(1, h, out_tgt)
    for h in range(2):
        drain(red_sem.at[1, h, 2, 0], stage1.at[h, peers])


def per_device(
    source_points, target_points, source_logw, target_logw, warm_start, pairs, owner_slot
):
    groups = lax.axis_size("blk")
    side = round(lax.axis_size("pair") ** 0.5)
    points = source_logw.shape[0]
    nb = points // BS
    capacity = pairs.shape[-1] // groups
    entries = groups * capacity
    rows = groups * GROUP_ROWS
    seg = nb // side
    reductions = 2 * ITERS - 1
    slots = -(-owner_slot.shape[0] // 2048) * 2048
    owner = jnp.pad(owner_slot, (0, slots - owner_slot.shape[0])).reshape(-1, HALF)
    vmem = pl.BlockSpec(memory_space=pltpu.VMEM)
    out = jax.ShapeDtypeStruct((points // HALF, HALF), F32)
    dma = pltpu.SemaphoreType.DMA
    tall = 6 * GROUP_ROWS
    source_pot, target_pot = pl.pallas_call(
        functools.partial(kernel, groups, side, capacity, nb),
        out_shape=(out, out),
        in_specs=[vmem] * 2 + [pl.BlockSpec(memory_space=pl.ANY)] * 5,
        out_specs=(vmem, vmem),
        scratch_shapes=[
            pltpu.VMEM((3, points), F32),
            *[pltpu.VMEM((points // HALF, HALF), F32)] * 2,
            pltpu.VMEM((3, points), F32),
            pltpu.VMEM((points // HALF, HALF), F32),
            *[pltpu.VMEM((3, nb // GROUP_ROWS, GROUP_ROWS, BS), F32)] * 2,
            dma((5,)),
            *[pltpu.VMEM((groups, GROUP_ROWS, HALF), jnp.int32)] * 3,
            pltpu.VMEM((2, capacity, groups, HALF), jnp.int32),
            pltpu.VMEM((2, 2, side, GROUP_ROWS, HALF), jnp.int32),
            pltpu.VMEM((2, 2, side, nb, HALF), BF16),
            pltpu.VMEM((2, 2, side * entries, nb), BF16),
            *[pltpu.VMEM((rows, nb), BF16)] * 2,
            pltpu.VMEM((4, 3, nb, BS), BF16),
            pltpu.VMEM((3, groups, GROUP_ROWS, BS), F32),
            *[pltpu.VMEM((groups, 4, GROUP_ROWS, BS), F32)] * 2,
            *[pltpu.VMEM((entries, GROUP_ROWS, BS), F32)] * 2,
            *[pltpu.VMEM((entries, tall, BS), BF16)] * 3,
            *[pltpu.VMEM((2, groups, GROUP_ROWS, HALF), F32)] * 7,
            *[pltpu.VMEM((capacity, groups, HALF), F32)] * 2,
            *[pltpu.VMEM((ITERS, 2, groups, GROUP_ROWS, HALF), F32)] * 2,
            pltpu.VMEM((reductions, 2, capacity, groups, HALF), F32),
            pltpu.VMEM((reductions, 2, side, capacity, groups, HALF), F32),
            pltpu.VMEM((side, nb, HALF), F32),
            pltpu.VMEM((2, nb, HALF), F32),
            *[pltpu.VMEM((reductions, 2, side, capacity, groups, HALF), F32)] * 2,
            pltpu.VMEM((2, nb, HALF), F32),
            pltpu.VMEM((2, side, seg, HALF), F32),
            pltpu.VMEM((2, 2, side, seg, HALF), F32),
            pltpu.VMEM((2, 2, nb, HALF), F32),
            dma((2,)),
            dma((2, 2, 2)),
            dma,
            dma((groups,)),
            dma((2,)),
            dma((2, groups)),
            dma((ITERS, 2, 2)),
            dma((reductions, 2, 2, 2)),
            dma((2, 2, 3, 2)),
        ],
        compiler_params=pltpu.CompilerParams(
            collective_id=0, has_side_effects=True, vmem_limit_bytes=40 * 1024 * 1024
        ),
        name="sinkhorn",
    )(
        pairs[0, 0], owner,
        *[
            pltpu.with_memory_space_constraint(value, pltpu.HBM)
            for value in (
                target_points, target_logw.reshape(-1, HALF), warm_start.reshape(-1, HALF),
                source_points, source_logw.reshape(-1, HALF),
            )
        ],
    )
    return source_pot.reshape(-1), target_pot.reshape(-1)


def solution(mesh):
    return jax.shard_map(
        per_device,
        mesh=mesh,
        in_specs=(
            P(None, "blk"),
            P(None, "blk"),
            P("blk"),
            P("blk"),
            P("blk"),
            P("blk", "pair", None, None),
            P(),
        ),
        out_specs=(P("blk"), P("blk")),
        check_vma=False,
    )
```
